256 devices in a mesh: dp: 2 (over y_hi), ctx: 128 (over x, z, y_lo, core).
Axes of the slice: x: 4, y: 4 (y_hi: 2, y_lo: 2; y = y_hi * 2 + y_lo), z: 8, core: 2. Of those that a mesh axis runs over, the one named last changes fastest.
Arguments:
- projected: bfloat16 [3, 2, 16384, 4096], P(None, 'dp', 'ctx'), may hold values from -6 to 6
- short_taps: float32 [3, 3, 4096], replicated, may hold values from -3 to 3
- long_filter: float32 [4096, 16384], P('ctx'), may hold values from -3 to 3
- grad_out: bfloat16 [2, 16384, 4096], P('dp', 'ctx'), may hold values from -6 to 6
Outputs:
- grad_projected: bfloat16 [3, 2, 16384, 4096], P(None, 'dp', 'ctx')
- grad_taps: float32 [3, 3, 4096], replicated
- grad_filter: float32 [4096, 16384], P('ctx', 'dp')
The draws below stay inside these ranges and needn't reach their ends.
All inputs are finite; a program needn't handle non-finite values.
Results may differ from the reference program's by a relative error of at most 0.01.
Values may be sent and summed in bfloat16 or wider, within the bound.
No kernel may reach another device: no remote copies, remote signals or barrier semaphores. Data moves between devices by JAX's collectives and lax.ppermute only.
A program may use at most 192 MiB of HBM per device.

```python
import math
import jax
import jax.numpy as jnp
from jax import lax

C = 4096
SEQ = 16384
SEQS = 2


def draw_long_filter(key, part):
    key = jax.random.fold_in(key, 7)
    keys = jax.random.split(key, 5)
    lags = jnp.arange(SEQ, dtype=jnp.float32)[None, :]
    slow_share = 0.5
    coin = jax.random.uniform(keys[0], (C, 1), dtype=jnp.float32)
    slow_rate = jnp.exp(jax.random.uniform(keys[1], (C, 1), dtype=jnp.float32, minval=math.log(0.25 / SEQ), maxval=math.log(1.0 / SEQ)))
    fast_rate = jnp.exp(jax.random.uniform(keys[2], (C, 1), dtype=jnp.float32, minval=math.log(1.0 / SEQ), maxval=math.log(1.0 / 30.0)))
    decay_rate = jnp.where(coin < slow_share, slow_rate, fast_rate)
    noise = jax.random.truncated_normal(keys[3], -4.0, 4.0, (C, SEQ), dtype=jnp.float32)
    tail = noise * jnp.sqrt(2.0 * decay_rate) * jnp.exp(-decay_rate * lags)
    direct = jax.random.uniform(keys[4], (C, 1), dtype=jnp.float32, minval=0.5, maxval=1.5)
    return jnp.where(lags == 0.0, direct, tail).astype(jnp.float32)


def block_scale(own_key, shape, cuts, smallest, largest):
    loudness = 1.0
    for axis_at, shards_of in cuts:
        draws = jax.random.uniform(jax.random.fold_in(jax.random.fold_in(own_key, 6), axis_at), (shards_of,), jnp.float32, smallest / len(cuts), largest / len(cuts))
        loudness = loudness * jnp.repeat(jnp.exp(draws), shape[axis_at] // shards_of).reshape((-1,) + (1,) * (len(shape) - 1 - axis_at))
    return loudness


def centred(own_key, dims, deviation, limit, shards=(), kind=jnp.bfloat16):
    drawn = jax.random.normal(own_key, dims, jnp.float32) * deviation
    if len(shards) > 0:
        drawn = block_scale(own_key, dims, shards, -0.22, 0.18) * drawn
    return jnp.clip(drawn, min=-limit, max=limit).astype(kind)


def setup_inputs(seed: int = 0) -> dict:
    key_list = jax.random.split(jax.random.key(seed), 5)
    return {
        "projected": centred(key_list[0], (3, SEQS, SEQ, C), 1.0, 6.0, ((1, 2), (2, 128))),
        "short_taps": centred(key_list[1], (3, 3, C), 0.6, 3.0, (), jnp.float32),
        "long_filter": draw_long_filter(jax.random.fold_in(key_list[4], 71), 0),
        "grad_out": centred(key_list[3], (SEQS, SEQ, C), 1.0, 6.0, ((0, 2), (1, 128))),
    }


def block_terms(pieces):
    proj_block, tap_block, filter_block, grad_block = pieces
    proj_wide = proj_block.astype(jnp.float32)
    padded = jnp.pad(proj_wide, ((0, 0), (0, 0), (2, 0), (0, 0)))
    features = sum(tap_block[:, tap, None, None, :] * padded[:, :, 2 - tap:2 - tap + SEQ, :] for tap in range(3))
    grad_rows = grad_block.astype(jnp.float32)
    gated_rows = (features[1] * features[2]).astype(jnp.bfloat16)
    grad_gate = (grad_rows * features[0]).astype(jnp.bfloat16)
    fft_len = 2 * SEQ
    spec_gate = jnp.fft.rfft(gated_rows.astype(jnp.float32), n=fft_len, axis=1)
    spec_grad = jnp.fft.rfft(grad_gate.astype(jnp.float32), n=fft_len, axis=1)
    spec_filter = jnp.fft.rfft(filter_block.T, n=fft_len, axis=0)[None]
    conv_out = jnp.fft.irfft(spec_gate * spec_filter, n=fft_len, axis=1)[:, :SEQ].astype(jnp.bfloat16)
    corr_out = jnp.fft.irfft(jnp.conj(spec_filter) * spec_grad, n=fft_len, axis=1)[:, :SEQ].astype(jnp.bfloat16)
    lag_terms = jnp.fft.irfft(jnp.conj(spec_gate) * spec_grad, n=fft_len, axis=1)[:, :SEQ]
    lag_grad = jnp.sum(lag_terms, axis=0).T.astype(jnp.float32)
    conv_wide = conv_out.astype(jnp.float32)
    corr_wide = corr_out.astype(jnp.float32)
    grads = jnp.stack([grad_rows * conv_wide, corr_wide * features[2], corr_wide * features[1]])
    grads_padded = jnp.pad(grads, ((0, 0), (0, 0), (0, 2), (0, 0)))
    grad_in = sum(tap_block[:, tap, None, None, :] * grads_padded[:, :, tap:tap + SEQ, :] for tap in range(3))
    tap_grad = jnp.stack([jnp.sum(grads * padded[:, :, 2 - tap:2 - tap + SEQ, :], axis=(1, 2)) for tap in range(3)], axis=1)
    return grad_in.astype(jnp.bfloat16), tap_grad, lag_grad


def reference(projected, short_taps, long_filter, grad_out):
    width_block = math.gcd(C, 128)
    blocks = C // width_block
    proj_blocks = jnp.moveaxis(projected.reshape(3, SEQS, SEQ, blocks, width_block), 3, 0)
    tap_blocks = jnp.moveaxis(short_taps.reshape(3, 3, blocks, width_block), 2, 0)
    filter_blocks = long_filter.reshape(blocks, width_block, SEQ)
    grad_blocks = jnp.moveaxis(grad_out.reshape(SEQS, SEQ, blocks, width_block), 2, 0)
    grad_in, tap_grad, lag_grad = lax.map(block_terms, (proj_blocks, tap_blocks, filter_blocks, grad_blocks))
    grad_projected = jnp.moveaxis(grad_in, 0, 3).reshape(3, SEQS, SEQ, C)
    grad_taps = jnp.moveaxis(tap_grad, 0, 2).reshape(3, 3, C)
    grad_filter = lag_grad.reshape(C, SEQ)
    return grad_projected, grad_taps, grad_filter
```

```python
import functools
import math

import jax
import jax.numpy as jnp
import numpy as np
from jax import lax
from jax.experimental import pallas as pl
from jax.experimental.pallas import tpu as pltpu
from jax.sharding import PartitionSpec as P

ROWS = 128
MIB = 2**20


def rounded(table):
    high = table.astype(jnp.bfloat16)
    low = (table - high.astype(np.float64)).astype(jnp.bfloat16)
    return high, low


@functools.cache
def tables():
    idx = np.arange(ROWS, dtype=np.float64)
    quarter = idx + 0.25
    ang_a = 2.0 * math.pi * np.outer(quarter, idx) / ROWS
    fwd_a = np.concatenate([np.cos(ang_a), -np.sin(ang_a)], axis=0)
    inv_a = np.concatenate([np.cos(ang_a.T), -np.sin(ang_a.T)], axis=1) / ROWS**2
    ang_w = 2.0 * math.pi * np.outer(quarter, idx) / ROWS**2
    turn = np.stack([np.cos(ang_w), -np.sin(ang_w)]).astype(np.float32)
    ang_b = 2.0 * math.pi * (np.outer(idx, idx) % ROWS) / ROWS
    cos_b, sin_b = np.cos(ang_b), np.sin(ang_b)
    fwd_b = np.block([[cos_b, -sin_b], [sin_b, cos_b]])
    inv_b = np.block([[cos_b, sin_b], [-sin_b, cos_b]])
    return {
        "fwd_a": np.concatenate(rounded(fwd_a), axis=1),
        "turn": turn,
        "fwd_b": np.stack(rounded(fwd_b)),
        "inv_b": np.stack(rounded(inv_b)),
        "inv_a": np.stack(rounded(inv_a)),
    }


def dot(lhs, rhs):
    return lax.dot_general(lhs, rhs, (((1,), (0,)), ((), ())), preferred_element_type=jnp.float32)


def split(value):
    high = value.astype(jnp.bfloat16)
    return high, (value - high.astype(jnp.float32)).astype(jnp.bfloat16)


def halves(value):
    return value[:, :ROWS], value[:, ROWS:]


def params(mib=48):
    return pltpu.CompilerParams(vmem_limit_bytes=mib * MIB)


def shifted(ext_ref, stream, tap):
    return ext_ref[stream, pl.ds(8 - tap, ROWS), :]


def fill_ext(ext_ref, proj_ref, edge_ref):
    for stream in range(3):
        ext_ref[stream, pl.ds(8, ROWS), :] = proj_ref[stream].astype(jnp.float32)
        ext_ref[stream, pl.ds(6, 2), :] = edge_ref[pl.ds(2 * stream, 2), :]


def feature(ext_ref, taps_ref, stream):
    total = taps_ref[stream, pl.ds(0, 1), :] * shifted(ext_ref, stream, 0)
    for tap in (1, 2):
        total += taps_ref[stream, pl.ds(tap, 1), :] * shifted(ext_ref, stream, tap)
    return total


def edge_kernel(proj_ref, out_ref):
    out_ref[...] = jnp.zeros_like(out_ref)
    for stream in range(3):
        tail = proj_ref[stream].astype(jnp.float32)
        out_ref[pl.ds(2 * stream, 2), :] = tail[14:16, :]


def edges(proj):
    channels = proj.shape[-1]
    return pl.pallas_call(
        edge_kernel,
        grid=(1,),
        in_specs=[pl.BlockSpec((3, 16, channels), lambda i: (0, ROWS // 16 - 1, 0))],
        out_specs=pl.BlockSpec((8, channels), lambda i: (0, 0)),
        out_shape=jax.ShapeDtypeStruct((8, channels), jnp.float32),
        compiler_params=params(16),
    )(proj)


def gate_kernel(proj_ref, edge_ref, taps_ref, grad_ref, out_ref, ext_ref):
    fill_ext(ext_ref, proj_ref, edge_ref)
    query, key, value = (feature(ext_ref, taps_ref, stream) for stream in range(3))
    gated = key * value
    grad_gate = grad_ref[...].astype(jnp.float32) * query
    count, _, width, _ = out_ref.shape
    for at, rows in enumerate((gated, grad_gate)):
        out_ref[:, at] = rows.T.astype(jnp.bfloat16).reshape(count, width, ROWS)


def gates(proj, edge, taps, grad_out, width):
    channels = proj.shape[-1]
    block = min(512, channels)
    return pl.pallas_call(
        gate_kernel,
        grid=(channels // block,),
        in_specs=[
            pl.BlockSpec((3, ROWS, block), lambda i: (0, 0, i)),
            pl.BlockSpec((8, block), lambda i: (0, i)),
            pl.BlockSpec((3, 3, block), lambda i: (0, 0, i)),
            pl.BlockSpec((ROWS, block), lambda i: (0, i)),
        ],
        out_specs=pl.BlockSpec((block // width, 2, width, ROWS), lambda i: (i, 0, 0, 0)),
        out_shape=jax.ShapeDtypeStruct((channels // width, 2, width, ROWS), jnp.bfloat16),
        scratch_shapes=[pltpu.VMEM((3, ROWS + 8, block), jnp.float32)],
        compiler_params=params(32),
    )(proj, edge, taps, grad_out)


def spectrum_kernel(filter_ref, fwd_a_ref, turn_ref, fwd_b_ref, out_ref):
    cos_w, sin_w = turn_ref[0], turn_ref[1]

    def one(ch, carry):
        high, low = split(filter_ref[ch])
        y = dot(fwd_a_ref[...], jnp.concatenate([high, high], axis=0))
        y += dot(fwd_a_ref[...], jnp.concatenate([low, low], axis=0))
        y_re, y_im = y[:ROWS], y[ROWS:]
        turned = jnp.concatenate(
            [y_re * cos_w - y_im * sin_w, y_re * sin_w + y_im * cos_w], axis=1
        )
        high, low = split(turned)
        out_ref[ch] = dot(high, fwd_b_ref[0]) + dot(high, fwd_b_ref[1]) + dot(low, fwd_b_ref[0])
        return carry

    lax.fori_loop(0, filter_ref.shape[0], one, 0, unroll=2)


def whole(shape):
    return pl.BlockSpec(shape, lambda i: (0,) * len(shape))


def spectrum(filter_sq, tab):
    width = filter_sq.shape[0]
    block = min(8, width)
    return pl.pallas_call(
        spectrum_kernel,
        grid=(width // block,),
        in_specs=[
            pl.BlockSpec((block, ROWS, ROWS), lambda i: (i, 0, 0)),
            whole((2 * ROWS, 2 * ROWS)),
            whole((2, ROWS, ROWS)),
            whole((2, 2 * ROWS, 2 * ROWS)),
        ],
        out_specs=pl.BlockSpec((block, ROWS, 2 * ROWS), lambda i: (i, 0, 0)),
        out_shape=jax.ShapeDtypeStruct((width, ROWS, 2 * ROWS), jnp.float32),
        compiler_params=params(32),
        cost_estimate=pl.CostEstimate(
            flops=width * 5 * 2 * (2 * ROWS) ** 3, bytes_accessed=width * 3 * 4 * ROWS**2,
            transcendentals=0,
        ),
    )(filter_sq, tab["fwd_a"], tab["turn"], tab["fwd_b"])


def conv_kernel(
    in_ref, spec_ref, fwd_a_ref, turn_ref, fwd_b_ref, inv_b_ref, inv_a_ref,
    out_ref, lag_ref, rows_ref, *, group,
):
    block = in_ref.shape[2]
    for at in range(2):
        rows_ref[at] = in_ref[:, at].astype(jnp.float32).reshape(ROWS * block, ROWS)
    cos_w, sin_w = turn_ref[0], turn_ref[1]

    def one(ch):
        strided = pl.ds(ch, ROWS, stride=block)
        both = jnp.concatenate(
            [rows_ref[at, strided, :].astype(jnp.bfloat16) for at in range(2)], axis=1
        )
        y = dot(fwd_a_ref[...], jnp.concatenate([both, both], axis=0))
        stacked = []
        for at in range(2):
            y_re = y[:ROWS, at * ROWS : (at + 1) * ROWS]
            y_im = y[ROWS:, at * ROWS : (at + 1) * ROWS]
            stacked.append(
                jnp.concatenate(
                    [
                        (y_re * cos_w - y_im * sin_w).astype(jnp.bfloat16),
                        (y_re * sin_w + y_im * cos_w).astype(jnp.bfloat16),
                    ],
                    axis=1,
                )
            )
        stacked = jnp.concatenate(stacked, axis=0)
        z = dot(stacked, fwd_b_ref[0]) + dot(stacked, fwd_b_ref[1])
        x_re, x_im = halves(z[:ROWS])
        g_re, g_im = halves(z[ROWS:])
        h_re, h_im = halves(spec_ref[ch])
        products = jnp.concatenate(
            [
                jnp.concatenate([re.astype(jnp.bfloat16), im.astype(jnp.bfloat16)], axis=1)
                for re, im in (
                    (x_re * h_re - x_im * h_im, x_re * h_im + x_im * h_re),
                    (h_re * g_re + h_im * g_im, h_re * g_im - h_im * g_re),
                    (g_re * x_re + g_im * x_im, g_im * x_re - g_re * x_im),
                )
            ],
            axis=0,
        )
        v = dot(products, inv_b_ref[0]) + dot(products, inv_b_ref[1])
        parts_re, parts_im = [], []
        for at in range(3):
            v_re, v_im = halves(v[at * ROWS : (at + 1) * ROWS])
            parts_re.append((v_re * cos_w + v_im * sin_w).astype(jnp.bfloat16))
            parts_im.append((v_im * cos_w - v_re * sin_w).astype(jnp.bfloat16))
        turned = jnp.concatenate(
            [jnp.concatenate(parts_re, axis=1), jnp.concatenate(parts_im, axis=1)], axis=0
        )
        res = dot(inv_a_ref[0], turned) + dot(inv_a_ref[1], turned)
        for at in range(2):
            rows_ref[at, strided, :] = res[:, at * ROWS : (at + 1) * ROWS]
        lag_ref[ch] = res[:, 2 * ROWS :]

    def some(step, carry):
        for at in range(group):
            one(step * group + at)
        return carry

    lax.fori_loop(0, block // group, some, 0)
    for at in range(2):
        out_ref[:, at] = rows_ref[at].astype(jnp.bfloat16).reshape(ROWS, block, ROWS)


def convolve(received, spec, tab):
    width = received.shape[2]
    block = min(16, width)
    return pl.pallas_call(
        functools.partial(conv_kernel, group=2),
        grid=(width // block,),
        in_specs=[
            pl.BlockSpec((ROWS, 2, block, ROWS), lambda i: (0, 0, i, 0)),
            pl.BlockSpec((block, ROWS, 2 * ROWS), lambda i: (i, 0, 0)),
            whole((2 * ROWS, 2 * ROWS)),
            whole((2, ROWS, ROWS)),
            whole((2, 2 * ROWS, 2 * ROWS)),
            whole((2, 2 * ROWS, 2 * ROWS)),
            whole((2, ROWS, 2 * ROWS)),
        ],
        out_specs=[
            pl.BlockSpec((ROWS, 2, block, ROWS), lambda i: (0, 0, i, 0)),
            pl.BlockSpec((block, ROWS, ROWS), lambda i: (i, 0, 0)),
        ],
        out_shape=[
            jax.ShapeDtypeStruct((ROWS, 2, width, ROWS), jnp.bfloat16),
            jax.ShapeDtypeStruct((width, ROWS, ROWS), jnp.float32),
        ],
        scratch_shapes=[pltpu.VMEM((2, ROWS * block, ROWS), jnp.float32)],
        compiler_params=params(56),
    )(received, spec, tab["fwd_a"], tab["turn"], tab["fwd_b"], tab["inv_b"], tab["inv_a"])


def grads_kernel(
    ret_ref, proj_ref, edge_ref, taps_ref, grad_ref,
    out_ref, sums_ref, first_ref, last_ref, ext_ref, grads_ref,
):
    fill_ext(ext_ref, proj_ref, edge_ref)
    block = grad_ref.shape[1]
    conv, corr = (
        ret_ref[:, at].reshape(block, ROWS).astype(jnp.float32).T for at in range(2)
    )
    key, value = (feature(ext_ref, taps_ref, stream) for stream in (1, 2))
    grads = (grad_ref[...].astype(jnp.float32) * conv, corr * value, corr * key)
    first_ref[...] = jnp.zeros_like(first_ref)
    for stream in range(3):
        grads_ref[stream, pl.ds(0, ROWS), :] = grads[stream]
        grads_ref[stream, pl.ds(ROWS, 8), :] = jnp.zeros((8, block), jnp.float32)
        first_ref[pl.ds(2 * stream, 2), :] = grads[stream][:2]
        for tap in range(3):
            sums = jnp.sum(grads[stream] * shifted(ext_ref, stream, tap), axis=0, keepdims=True)
            sums_ref[pl.ds(3 * stream + tap, 1)] = sums.reshape(1, block // ROWS, ROWS)
        total = taps_ref[stream, pl.ds(0, 1), :] * grads[stream]
        for tap in (1, 2):
            total += taps_ref[stream, pl.ds(tap, 1), :] * grads_ref[stream, pl.ds(tap, ROWS), :]
        out_ref[stream] = total.astype(jnp.bfloat16)
        last_ref[stream] = total[ROWS - 16 :]


def stream_grads(returned, proj, edge, taps, grad_out):
    channels = proj.shape[-1]
    width = returned.shape[2]
    block = min(1024, channels)
    return pl.pallas_call(
        grads_kernel,
        grid=(channels // block,),
        in_specs=[
            pl.BlockSpec((block // width, 2, width, ROWS), lambda i: (i, 0, 0, 0)),
            pl.BlockSpec((3, ROWS, block), lambda i: (0, 0, i)),
            pl.BlockSpec((8, block), lambda i: (0, i)),
            pl.BlockSpec((3, 3, block), lambda i: (0, 0, i)),
            pl.BlockSpec((ROWS, block), lambda i: (0, i)),
        ],
        out_specs=[
            pl.BlockSpec((3, ROWS, block), lambda i: (0, 0, i)),
            pl.BlockSpec((9, block // ROWS, ROWS), lambda i: (0, i, 0)),
            pl.BlockSpec((8, block), lambda i: (0, i)),
            pl.BlockSpec((3, 16, block), lambda i: (0, 0, i)),
        ],
        out_shape=[
            jax.ShapeDtypeStruct((3, ROWS, channels), jnp.bfloat16),
            jax.ShapeDtypeStruct((9, channels // ROWS, ROWS), jnp.float32),
            jax.ShapeDtypeStruct((8, channels), jnp.float32),
            jax.ShapeDtypeStruct((3, 16, channels), jnp.float32),
        ],
        scratch_shapes=[
            pltpu.VMEM((3, ROWS + 8, block), jnp.float32),
            pltpu.VMEM((3, ROWS + 8, block), jnp.float32),
        ],
        compiler_params=params(48),
    )(returned, proj, edge, taps, grad_out)


def last_kernel(whole_ref, last_ref, later_ref, taps_ref, out_ref):
    del whole_ref
    for stream in range(3):
        later = later_ref[pl.ds(2 * stream, 2), :]
        tap_1, tap_2 = (taps_ref[stream, pl.ds(tap, 1), :] for tap in (1, 2))
        rows = last_ref[stream]
        row_14 = rows[14:15] + tap_2 * later[:1]
        row_15 = rows[15:] + tap_1 * later[:1] + tap_2 * later[1:]
        out_ref[stream] = jnp.concatenate([rows[:14], row_14, row_15], axis=0).astype(jnp.bfloat16)


def finish_rows(grad_rows, last, later, taps):
    channels = grad_rows.shape[-1]
    return pl.pallas_call(
        last_kernel,
        grid=(1,),
        in_specs=[
            pl.BlockSpec(memory_space=pl.ANY),
            whole((3, 16, channels)),
            whole((8, channels)),
            whole((3, 3, channels)),
        ],
        out_specs=pl.BlockSpec((3, 16, channels), lambda i: (0, ROWS // 16 - 1, 0)),
        out_shape=jax.ShapeDtypeStruct(grad_rows.shape, grad_rows.dtype),
        input_output_aliases={0: 0},
        compiler_params=params(16),
    )(grad_rows, last, later, taps)


def passed_along(value, steps):
    count = lax.axis_size("ctx")
    initial, last = (max(0, -steps), min(count, count - steps))
    return lax.ppermute(value, "ctx", [(source, source + steps) for source in range(initial, last)])


def exchanged(value, axes):
    return lax.all_to_all(value, axes, split_axis=0, concat_axis=0, tiled=True)


def sum_everywhere(sums):
    taps, blocks, _ = sums.shape
    devices = lax.axis_size("dp") * lax.axis_size("ctx")
    owners = taps * blocks // 2
    pieces = jnp.pad(sums.reshape(owners, 2, ROWS), ((0, devices - owners), (0, 0), (0, 0)))
    own = jnp.sum(exchanged(pieces, ("dp", "ctx")), axis=0)
    spread = exchanged(jnp.broadcast_to(own[None], (devices, 2, ROWS)), ("dp", "ctx"))
    return spread[:owners].reshape(3, 3, blocks * ROWS)


def local(projected, short_taps, long_filter, grad_out):
    tab = tables()
    proj = projected[:, 0]
    grad_rows = grad_out[0]
    width = long_filter.shape[0]
    edge = passed_along(edges(proj), 1)
    sent = gates(proj, edge, short_taps, grad_rows, width)
    received = exchanged(sent, "ctx")
    spec = spectrum(long_filter.reshape(width, ROWS, ROWS), tab)
    results, lag = convolve(received, spec, tab)
    returned = exchanged(results, "ctx")
    second = lax.axis_index("dp") == 1
    lower, upper = lag[:, : ROWS // 2], lag[:, ROWS // 2 :]
    other = lax.ppermute(
        jnp.where(second, lower, upper).astype(jnp.bfloat16), "dp", [(0, 1), (1, 0)]
    )
    lag_sum = jnp.where(second, upper, lower) + other.astype(jnp.float32)
    grad_filter = lag_sum.reshape(width, ROWS // 2 * ROWS)
    grad_in, sums, first, last = stream_grads(returned, proj, edge, short_taps, grad_rows)
    later = passed_along(first, -1)
    grad_in = finish_rows(grad_in, last, later, short_taps)
    return (grad_in[:, None], sum_everywhere(sums), grad_filter)


def solution(mesh):
    return jax.shard_map(
        local,
        mesh=mesh,
        in_specs=(P(None, "dp", "ctx", None), P(), P("ctx", None), P("dp", "ctx", None)),
        out_specs=(P(None, "dp", "ctx", None), P(), P("ctx", "dp")),
        check_vma=False,
    )
```

```python
import functools
import math

import jax
import jax.numpy as jnp
import numpy as np
from jax import lax
from jax.experimental import pallas as pl
from jax.experimental.pallas import tpu as pltpu
from jax.sharding import PartitionSpec as P

ROWS = 128
MIB = 2**20


def rounded(table):
    high = table.astype(jnp.bfloat16)
    low = (table - high.astype(np.float64)).astype(jnp.bfloat16)
    return high, low


@functools.cache
def tables():
    idx = np.arange(ROWS, dtype=np.float64)
    quarter = idx + 0.25
    ang_a = 2.0 * math.pi * np.outer(quarter, idx) / ROWS
    fwd_a = np.concatenate([np.cos(ang_a), -np.sin(ang_a)], axis=0)
    inv_a = np.concatenate([np.cos(ang_a.T), -np.sin(ang_a.T)], axis=1) / ROWS**2
    ang_w = 2.0 * math.pi * np.outer(quarter, idx) / ROWS**2
    turn = np.stack([np.cos(ang_w), -np.sin(ang_w)]).astype(np.float32)
    ang_b = 2.0 * math.pi * (np.outer(idx, idx) % ROWS) / ROWS
    cos_b, sin_b = np.cos(ang_b), np.sin(ang_b)
    fwd_b = np.block([[cos_b, -sin_b], [sin_b, cos_b]])
    inv_b = np.block([[cos_b, sin_b], [-sin_b, cos_b]])
    return {
        "fwd_a": np.concatenate(rounded(fwd_a), axis=1),
        "turn": turn,
        "fwd_b": np.stack(rounded(fwd_b)),
        "fwd_b_high": np.stack(rounded(fwd_b)[:1]),
        "inv_b": np.stack(rounded(inv_b)),
        "inv_b_high": np.stack(rounded(inv_b)[:1]),
        "inv_a": np.stack(rounded(inv_a)),
        "inv_a_high": np.stack(rounded(inv_a)[:1]),
    }


def dot(lhs, rhs):
    return lax.dot_general(lhs, rhs, (((1,), (0,)), ((), ())), preferred_element_type=jnp.float32)


def split(value):
    high = value.astype(jnp.bfloat16)
    return high, (value - high.astype(jnp.float32)).astype(jnp.bfloat16)


def halves(value):
    return value[:, :ROWS], value[:, ROWS:]


def held(value):
    return pltpu.with_memory_space_constraint(value, pltpu.HBM)


def params(mib=48):
    return pltpu.CompilerParams(vmem_limit_bytes=mib * MIB)


def shifted(ext_ref, stream, tap):
    return ext_ref[stream, pl.ds(8 - tap, ROWS), :]


def fill_ext(ext_ref, proj_ref, edge_ref):
    for stream in range(3):
        ext_ref[stream, pl.ds(8, ROWS), :] = proj_ref[stream].astype(jnp.float32)
        ext_ref[stream, pl.ds(6, 2), :] = edge_ref[pl.ds(2 * stream, 2), :]


def feature(ext_ref, taps_ref, stream):
    total = taps_ref[stream, pl.ds(0, 1), :] * shifted(ext_ref, stream, 0)
    for tap in (1, 2):
        total += taps_ref[stream, pl.ds(tap, 1), :] * shifted(ext_ref, stream, tap)
    return total


def edge_kernel(proj_ref, out_ref):
    out_ref[...] = jnp.zeros_like(out_ref)
    for stream in range(3):
        tail = proj_ref[stream].astype(jnp.float32)
        out_ref[pl.ds(2 * stream, 2), :] = tail[14:16, :]


def edges(proj):
    channels = proj.shape[-1]
    return pl.pallas_call(
        edge_kernel,
        grid=(1,),
        in_specs=[pl.BlockSpec((3, 16, channels), lambda i: (0, ROWS // 16 - 1, 0))],
        out_specs=pl.BlockSpec((8, channels), lambda i: (0, 0)),
        out_shape=jax.ShapeDtypeStruct((8, channels), jnp.float32),
        compiler_params=params(16),
    )(held(proj))


def gate_kernel(proj_ref, edge_ref, taps_ref, grad_ref, out_ref, ext_ref):
    fill_ext(ext_ref, proj_ref, edge_ref)
    query, key, value = (feature(ext_ref, taps_ref, stream) for stream in range(3))
    gated = key * value
    grad_gate = grad_ref[...].astype(jnp.float32) * query
    count, _, width, _ = out_ref.shape
    for at, rows in enumerate((gated, grad_gate)):
        out_ref[:, at] = rows.astype(jnp.bfloat16).T.reshape(count, width, ROWS)


def gates(proj, edge, taps, grad_out, width):
    channels = proj.shape[-1]
    block = min(1024, channels)
    return pl.pallas_call(
        gate_kernel,
        grid=(channels // block,),
        in_specs=[
            pl.BlockSpec((3, ROWS, block), lambda i: (0, 0, i)),
            pl.BlockSpec((8, block), lambda i: (0, i)),
            pl.BlockSpec((3, 3, block), lambda i: (0, 0, i)),
            pl.BlockSpec((ROWS, block), lambda i: (0, i)),
        ],
        out_specs=pl.BlockSpec((block // width, 2, width, ROWS), lambda i: (i, 0, 0, 0)),
        out_shape=jax.ShapeDtypeStruct((channels // width, 2, width, ROWS), jnp.bfloat16),
        scratch_shapes=[pltpu.VMEM((3, ROWS + 8, block), jnp.float32)],
        compiler_params=params(32),
    )(held(proj), edge, taps, held(grad_out))


def spectrum_kernel(filter_ref, fwd_a_ref, turn_ref, fwd_b_ref, out_ref):
    cos_w, sin_w = turn_ref[0], turn_ref[1]

    def one(ch, carry):
        high, low = split(filter_ref[ch])
        y = dot(fwd_a_ref[...], jnp.concatenate([high, high], axis=0))
        y += dot(fwd_a_ref[...], jnp.concatenate([low, low], axis=0))
        y_re, y_im = y[:ROWS], y[ROWS:]
        turned = jnp.concatenate(
            [y_re * cos_w - y_im * sin_w, y_re * sin_w + y_im * cos_w], axis=1
        )
        high, low = split(turned)
        out_ref[ch] = dot(high, fwd_b_ref[0]) + dot(high, fwd_b_ref[1]) + dot(low, fwd_b_ref[0])
        return carry

    lax.fori_loop(0, filter_ref.shape[0], one, 0, unroll=2)


def whole(shape):
    return pl.BlockSpec(shape, lambda i: (0,) * len(shape))


def spectrum(filter_sq, tab):
    width = filter_sq.shape[0]
    block = min(8, width)
    return pl.pallas_call(
        spectrum_kernel,
        grid=(width // block,),
        in_specs=[
            pl.BlockSpec((block, ROWS, ROWS), lambda i: (i, 0, 0)),
            whole((2 * ROWS, 2 * ROWS)),
            whole((2, ROWS, ROWS)),
            whole((2, 2 * ROWS, 2 * ROWS)),
        ],
        out_specs=pl.BlockSpec((block, ROWS, 2 * ROWS), lambda i: (i, 0, 0)),
        out_shape=pltpu.HBM((width, ROWS, 2 * ROWS), jnp.float32),
        compiler_params=params(32),
        cost_estimate=pl.CostEstimate(
            flops=width * 5 * 2 * (2 * ROWS) ** 3, bytes_accessed=width * 3 * 4 * ROWS**2,
            transcendentals=0,
        ),
    )(filter_sq, tab["fwd_a"], tab["turn"], tab["fwd_b"])


def apply_right(rows, table_ref):
    total = dot(rows, table_ref[0])
    for term in range(1, table_ref.shape[0]):
        total += dot(rows, table_ref[term])
    return total


def apply_left(table_ref, columns):
    total = dot(table_ref[0], columns)
    for term in range(1, table_ref.shape[0]):
        total += dot(table_ref[term], columns)
    return total


def side(left, right):
    return jnp.concatenate([left.astype(jnp.bfloat16), right.astype(jnp.bfloat16)], axis=1)


def turned_back(spectra, inv_b_ref, inv_a_ref, cos_w, sin_w):
    v = apply_right(spectra, inv_b_ref)
    parts_re, parts_im = [], []
    for at in range(spectra.shape[0] // ROWS):
        v_re, v_im = halves(v[at * ROWS : (at + 1) * ROWS])
        parts_re.append((v_re * cos_w + v_im * sin_w).astype(jnp.bfloat16))
        parts_im.append((v_im * cos_w - v_re * sin_w).astype(jnp.bfloat16))
    parts = [jnp.concatenate(parts_re, axis=1), jnp.concatenate(parts_im, axis=1)]
    return apply_left(inv_a_ref, jnp.concatenate(parts, axis=0))


def conv_kernel(
    in_ref, spec_ref, fwd_a_ref, turn_ref, fwd_b_ref, inv_b_ref, inv_a_ref,
    out_ref, lag_ref, rows_ref, outs_ref, *, group,
):
    block = in_ref.shape[2]
    for at in range(2):
        rows_ref[at] = in_ref[:, at].astype(jnp.float32).reshape(ROWS * block, ROWS)
    cos_w, sin_w = turn_ref[0], turn_ref[1]

    def some(step, carry):
        chans = [step * group + at for at in range(group)]
        places = [(at, pl.ds(ch, ROWS, stride=block)) for ch in chans for at in range(2)]
        rows = [rows_ref[at, strided, :].astype(jnp.bfloat16) for at, strided in places]
        columns = jnp.concatenate(rows, axis=1)
        y = dot(fwd_a_ref[...], jnp.concatenate([columns, columns], axis=0))
        turned = []
        for at in range(2 * group):
            y_re = y[:ROWS, at * ROWS : (at + 1) * ROWS]
            y_im = y[ROWS:, at * ROWS : (at + 1) * ROWS]
            turned.append(side(y_re * cos_w - y_im * sin_w, y_re * sin_w + y_im * cos_w))
        z = apply_right(jnp.concatenate(turned, axis=0), fwd_b_ref)
        products = []
        for at, ch in enumerate(chans):
            x_re, x_im = halves(z[2 * at * ROWS : (2 * at + 1) * ROWS])
            g_re, g_im = halves(z[(2 * at + 1) * ROWS : (2 * at + 2) * ROWS])
            h_re, h_im = halves(spec_ref[ch])
            lag_ref[ch] = side(g_re * x_re + g_im * x_im, g_im * x_re - g_re * x_im)
            products.append(side(x_re * h_re - x_im * h_im, x_re * h_im + x_im * h_re))
            products.append(side(h_re * g_re + h_im * g_im, h_re * g_im - h_im * g_re))
        res = turned_back(jnp.concatenate(products, axis=0), inv_b_ref, inv_a_ref, cos_w, sin_w)
        for column, (at, strided) in enumerate(places):
            outs_ref[at, strided, :] = res[:, column * ROWS : (column + 1) * ROWS]
        return carry

    lax.fori_loop(0, block // group, some, 0)
    for at in range(2):
        out_ref[:, at] = outs_ref[at].astype(jnp.bfloat16).reshape(ROWS, block, ROWS)


def convolve(received, spec, tab, group=8, block=16):
    width = received.shape[2]
    names = ("fwd_a", "turn", "fwd_b_high", "inv_b_high", "inv_a_high")
    return pl.pallas_call(
        functools.partial(conv_kernel, group=group),
        grid=(width // block,),
        in_specs=[
            pl.BlockSpec((ROWS, 2, block, ROWS), lambda i: (0, 0, i, 0)),
            pl.BlockSpec((block, ROWS, 2 * ROWS), lambda i: (i, 0, 0)),
        ]
        + [whole(tab[name].shape) for name in names],
        out_specs=[
            pl.BlockSpec((ROWS, 2, block, ROWS), lambda i: (0, 0, i, 0)),
            pl.BlockSpec((block, ROWS, 2 * ROWS), lambda i: (i, 0, 0)),
        ],
        out_shape=[
            pltpu.HBM((ROWS, 2, width, ROWS), jnp.bfloat16),
            pltpu.HBM((width, ROWS, 2 * ROWS), jnp.bfloat16),
        ],
        scratch_shapes=[pltpu.VMEM((2, ROWS * block, ROWS), jnp.float32)] * 2,
        compiler_params=params(40),
    )(received, held(spec), *(tab[name] for name in names))


def lag_kernel(products_ref, turn_ref, inv_b_ref, inv_a_ref, out_ref):
    count = products_ref.shape[0]
    products = products_ref[...].reshape(count * ROWS, 2 * ROWS)
    res = turned_back(products, inv_b_ref, inv_a_ref, turn_ref[0], turn_ref[1])
    for ch in range(count):
        out_ref[ch] = res[:, ch * ROWS : (ch + 1) * ROWS]


def lags(products, tab):
    width = products.shape[0]
    block = min(8, width)
    names = ("turn", "inv_b", "inv_a")
    return pl.pallas_call(
        lag_kernel,
        grid=(width // block,),
        in_specs=[pl.BlockSpec((block, ROWS, 2 * ROWS), lambda i: (i, 0, 0))]
        + [whole(tab[name].shape) for name in names],
        out_specs=pl.BlockSpec((block, ROWS, ROWS), lambda i: (i, 0, 0)),
        out_shape=jax.ShapeDtypeStruct((width, ROWS, ROWS), jnp.float32),
        compiler_params=params(32),
        cost_estimate=pl.CostEstimate(
            flops=width * 4 * 2 * (2 * ROWS) ** 3, bytes_accessed=width * 8 * ROWS**2,
            transcendentals=0,
        ),
    )(products, *(tab[name] for name in names))


def grads_kernel(
    ret_ref, proj_ref, edge_ref, taps_ref, grad_ref,
    out_ref, sums_ref, first_ref, last_ref, ext_ref, grads_ref,
):
    fill_ext(ext_ref, proj_ref, edge_ref)
    block = grad_ref.shape[1]
    conv, corr = (
        ret_ref[:, at].reshape(block, ROWS).T.astype(jnp.float32) for at in range(2)
    )
    key, value = (feature(ext_ref, taps_ref, stream) for stream in (1, 2))
    grads = (grad_ref[...].astype(jnp.float32) * conv, corr * value, corr * key)
    first_ref[...] = jnp.zeros_like(first_ref)
    sums_ref[...] = jnp.zeros_like(sums_ref)
    for stream in range(3):
        grads_ref[stream, pl.ds(0, ROWS), :] = grads[stream]
        grads_ref[stream, pl.ds(ROWS, 8), :] = jnp.zeros((8, block), jnp.float32)
        first_ref[pl.ds(2 * stream, 2), :] = grads[stream][:2]
        for tap in range(3):
            sums = jnp.sum(grads[stream] * shifted(ext_ref, stream, tap), axis=0, keepdims=True)
            sums_ref[pl.ds(3 * stream + tap, 1)] = sums.reshape(1, block // ROWS, ROWS)
        total = taps_ref[stream, pl.ds(0, 1), :] * grads[stream]
        for tap in (1, 2):
            total += taps_ref[stream, pl.ds(tap, 1), :] * grads_ref[stream, pl.ds(tap, ROWS), :]
        out_ref[stream] = total.astype(jnp.bfloat16)
        last_ref[stream] = total[ROWS - 16 :]


def stream_grads(returned, proj, edge, taps, grad_out):
    channels = proj.shape[-1]
    width = returned.shape[2]
    block = min(1024, channels)
    return pl.pallas_call(
        grads_kernel,
        grid=(channels // block,),
        in_specs=[
            pl.BlockSpec((block // width, 2, width, ROWS), lambda i: (i, 0, 0, 0)),
            pl.BlockSpec((3, ROWS, block), lambda i: (0, 0, i)),
            pl.BlockSpec((8, block), lambda i: (0, i)),
            pl.BlockSpec((3, 3, block), lambda i: (0, 0, i)),
            pl.BlockSpec((ROWS, block), lambda i: (0, i)),
        ],
        out_specs=[
            pl.BlockSpec((3, ROWS, block), lambda i: (0, 0, i)),
            pl.BlockSpec((16, block // ROWS, ROWS), lambda i: (0, i, 0)),
            pl.BlockSpec((8, block), lambda i: (0, i)),
            pl.BlockSpec((3, 16, block), lambda i: (0, 0, i)),
        ],
        out_shape=[
            jax.ShapeDtypeStruct((3, ROWS, channels), jnp.bfloat16),
            jax.ShapeDtypeStruct((16, channels // ROWS, ROWS), jnp.float32),
            pltpu.HBM((8, channels), jnp.float32),
            pltpu.HBM((3, 16, channels), jnp.float32),
        ],
        scratch_shapes=[
            pltpu.VMEM((3, ROWS + 8, block), jnp.float32),
            pltpu.VMEM((3, ROWS + 8, block), jnp.float32),
        ],
        compiler_params=params(48),
    )(returned, held(proj), edge, taps, held(grad_out))


def last_kernel(whole_ref, last_ref, later_ref, taps_ref, out_ref):
    del whole_ref
    for stream in range(3):
        later = later_ref[pl.ds(2 * stream, 2), :]
        tap_1, tap_2 = (taps_ref[stream, pl.ds(tap, 1), :] for tap in (1, 2))
        rows = last_ref[stream]
        row_14 = rows[14:15] + tap_2 * later[:1]
        row_15 = rows[15:] + tap_1 * later[:1] + tap_2 * later[1:]
        out_ref[stream] = jnp.concatenate([rows[:14], row_14, row_15], axis=0).astype(jnp.bfloat16)


def finish_rows(grad_rows, last, later, taps):
    channels = grad_rows.shape[-1]
    return pl.pallas_call(
        last_kernel,
        grid=(1,),
        in_specs=[
            pl.BlockSpec(memory_space=pl.ANY),
            whole((3, 16, channels)),
            whole((8, channels)),
            whole((3, 3, channels)),
        ],
        out_specs=pl.BlockSpec((3, 16, channels), lambda i: (0, ROWS // 16 - 1, 0)),
        out_shape=jax.ShapeDtypeStruct(grad_rows.shape, grad_rows.dtype),
        input_output_aliases={0: 0},
        compiler_params=params(16),
    )(grad_rows, last, later, taps)


def passed_along(value, steps):
    count = lax.axis_size("ctx")
    initial, last = (max(0, -steps), min(count, count - steps))
    return lax.ppermute(value, "ctx", [(source, source + steps) for source in range(initial, last)])


def exchanged(value, axes):
    return lax.all_to_all(value, axes, split_axis=0, concat_axis=0, tiled=True)


def sum_everywhere(sums):
    channels = sums.shape[1] * ROWS
    devices = lax.axis_size("dp") * lax.axis_size("ctx")
    pieces = sums.reshape(devices, 2, ROWS)
    own = jnp.sum(exchanged(pieces, ("dp", "ctx")), axis=0)
    spread = exchanged(jnp.broadcast_to(own[None], pieces.shape), ("dp", "ctx"))
    return spread.reshape(16, channels)[:9].reshape(3, 3, channels)


def local(projected, short_taps, long_filter, grad_out):
    tab = tables()
    proj = projected[:, 0]
    grad_rows = grad_out[0]
    width = long_filter.shape[0]
    edge = passed_along(edges(proj), 1)
    sent = gates(proj, edge, short_taps, grad_rows, width)
    received = exchanged(sent, "ctx")
    spec = spectrum(long_filter.reshape(width, ROWS, ROWS), tab)
    results, products = convolve(received, spec, tab)
    returned = exchanged(results, "ctx")
    lag = lags(products, tab)
    second = lax.axis_index("dp") == 1
    lower, upper = lag[:, : ROWS // 2], lag[:, ROWS // 2 :]
    other = lax.ppermute(
        jnp.where(second, lower, upper).astype(jnp.bfloat16), "dp", [(0, 1), (1, 0)]
    )
    lag_sum = jnp.where(second, upper, lower) + other.astype(jnp.float32)
    grad_filter = lag_sum.reshape(width, ROWS // 2 * ROWS)
    grad_in, sums, first, last = stream_grads(returned, proj, edge, short_taps, grad_rows)
    later = passed_along(first, -1)
    grad_in = finish_rows(grad_in, last, later, short_taps)
    return (grad_in[:, None], sum_everywhere(sums), grad_filter)


def solution(mesh):
    return jax.shard_map(
        local,
        mesh=mesh,
        in_specs=(P(None, "dp", "ctx", None), P(), P("ctx", None), P("dp", "ctx", None)),
        out_specs=(P(None, "dp", "ctx", None), P(), P("ctx", "dp")),
        check_vma=False,
    )
```

```python
import functools
import math

import jax
import jax.numpy as jnp
import numpy as np
from jax import lax
from jax.experimental import pallas as pl
from jax.experimental.pallas import tpu as pltpu
from jax.sharding import PartitionSpec as P

ROWS = 128
MIB = 2**20


def rounded(table):
    high = table.astype(jnp.bfloat16)
    low = (table - high.astype(np.float64)).astype(jnp.bfloat16)
    return high, low


@functools.cache
def tables():
    idx = np.arange(ROWS, dtype=np.float64)
    quarter = idx + 0.25
    ang_a = 2.0 * math.pi * np.outer(quarter, idx) / ROWS
    fwd_a = np.concatenate([np.cos(ang_a), -np.sin(ang_a)], axis=0)
    inv_a = np.concatenate([np.cos(ang_a.T), -np.sin(ang_a.T)], axis=1) / ROWS**2
    ang_w = 2.0 * math.pi * np.outer(quarter, idx) / ROWS**2
    turn = np.stack([np.cos(ang_w), -np.sin(ang_w)]).astype(np.float32)
    ang_b = 2.0 * math.pi * (np.outer(idx, idx) % ROWS) / ROWS
    cos_b, sin_b = np.cos(ang_b), np.sin(ang_b)
    fwd_b = np.block([[cos_b, -sin_b], [sin_b, cos_b]])
    inv_b = np.block([[cos_b, sin_b], [-sin_b, cos_b]])
    return {
        "fwd_a": np.concatenate(rounded(fwd_a), axis=1),
        "turn": turn,
        "fwd_b": np.stack(rounded(fwd_b)),
        "fwd_b_high": np.stack(rounded(fwd_b)[:1]),
        "inv_b": np.stack(rounded(inv_b)),
        "inv_b_high": np.stack(rounded(inv_b)[:1]),
        "inv_a": np.stack(rounded(inv_a)),
        "inv_a_high": np.stack(rounded(inv_a)[:1]),
    }


def dot(lhs, rhs):
    return lax.dot_general(lhs, rhs, (((1,), (0,)), ((), ())), preferred_element_type=jnp.float32)


def split(value):
    high = value.astype(jnp.bfloat16)
    return high, (value - high.astype(jnp.float32)).astype(jnp.bfloat16)


def halves(value):
    return value[:, :ROWS], value[:, ROWS:]


def held(value):
    return pltpu.with_memory_space_constraint(value, pltpu.HBM)


def params(mib=48):
    return pltpu.CompilerParams(vmem_limit_bytes=mib * MIB)


def fill_ext(ext_ref, proj_ref, edge_ref):
    for stream in range(3):
        ext_ref[stream, pl.ds(8, ROWS), :] = proj_ref[stream].astype(jnp.float32)
        ext_ref[stream, pl.ds(6, 2), :] = edge_ref[pl.ds(2 * stream, 2), :]


def edge_kernel(proj_ref, out_ref):
    out_ref[...] = jnp.zeros_like(out_ref)
    for stream in range(3):
        tail = proj_ref[stream].astype(jnp.float32)
        out_ref[pl.ds(2 * stream, 2), :] = tail[14:16, :]


def edges(proj):
    channels = proj.shape[-1]
    return pl.pallas_call(
        edge_kernel,
        grid=(1,),
        in_specs=[pl.BlockSpec((3, 16, channels), lambda i: (0, ROWS // 16 - 1, 0))],
        out_specs=pl.BlockSpec((8, channels), lambda i: (0, 0)),
        out_shape=jax.ShapeDtypeStruct((8, channels), jnp.float32),
        compiler_params=params(16),
    )(held(proj))


STEP = 32


def lanes_of(width):
    return [pl.ds(at, ROWS) for at in range(0, width, ROWS)]


def inputs_at(ext_ref, stream, row, lanes):
    rows = ext_ref[stream, pl.ds(row, STEP + 8), lanes]
    return [rows[8:]] + [pltpu.roll(rows, tap, 0)[8:] for tap in (1, 2)]


def filtered(taps_ref, stream, lanes, shifted):
    rows = taps_ref[stream, :, lanes]
    return sum(rows[tap : tap + 1] * shifted[tap] for tap in range(3))


def gate_kernel(proj_ref, taps_ref, grad_ref, out_ref, ext_ref):
    for stream in range(3):
        ext_ref[stream, pl.ds(8, ROWS), :] = proj_ref[stream].astype(jnp.float32)
        ext_ref[stream, pl.ds(0, 8), :] = jnp.zeros((8, grad_ref.shape[1]), jnp.float32)
    width = out_ref.shape[2]
    per = ROWS // width
    for at, lanes in enumerate(lanes_of(grad_ref.shape[1])):
        gated, grad_gate = [], []
        for row in range(0, ROWS, STEP):
            query, key, value = (
                filtered(taps_ref, stream, lanes, inputs_at(ext_ref, stream, row, lanes))
                for stream in range(3)
            )
            grad = grad_ref[pl.ds(row, STEP), lanes].astype(jnp.float32)
            gated.append((key * value).astype(jnp.bfloat16))
            grad_gate.append((grad * query).astype(jnp.bfloat16))
        for which, parts in enumerate((gated, grad_gate)):
            turned = jnp.concatenate(parts, axis=0).T
            out_ref[pl.ds(at * per, per), which] = turned.reshape(per, width, ROWS)


def gates(proj, taps, grad_out, width):
    channels = proj.shape[-1]
    block = min(2048, channels)
    return pl.pallas_call(
        gate_kernel,
        grid=(channels // block,),
        in_specs=[
            pl.BlockSpec((3, ROWS, block), lambda i: (0, 0, i)),
            pl.BlockSpec((3, 3, block), lambda i: (0, 0, i)),
            pl.BlockSpec((ROWS, block), lambda i: (0, i)),
        ],
        out_specs=pl.BlockSpec((block // width, 2, width, ROWS), lambda i: (i, 0, 0, 0)),
        out_shape=jax.ShapeDtypeStruct((channels // width, 2, width, ROWS), jnp.bfloat16),
        scratch_shapes=[pltpu.VMEM((3, ROWS + 8, block), jnp.float32)],
        compiler_params=params(32),
        cost_estimate=pl.CostEstimate(
            flops=40 * ROWS * channels, bytes_accessed=12 * ROWS * channels, transcendentals=0
        ),
    )(held(proj), taps, held(grad_out))


def head_kernel(rough_ref, proj_ref, edge_ref, taps_ref, grad_ref, out_ref):
    per, _, width, _ = out_ref.shape
    block = per * width
    features = []
    for stream in range(3):
        before = edge_ref[pl.ds(2 * stream, 2), :]
        rows = jnp.concatenate([before, proj_ref[stream].astype(jnp.float32)[:2]], axis=0)
        features.append(
            sum(taps_ref[stream, pl.ds(tap, 1), :] * rows[2 - tap : 4 - tap] for tap in range(3))
        )
    query, key, value = features
    grad = grad_ref[...].astype(jnp.float32)[:2]
    below = jnp.zeros((ROWS - 2, block), jnp.float32)
    head = lax.broadcasted_iota(jnp.int32, (block, ROWS), 1) < 2
    for which, rows in enumerate((key * value, grad * query)):
        turned = jnp.concatenate([rows, below], axis=0).astype(jnp.bfloat16).T
        kept = rough_ref[:, which].reshape(block, ROWS)
        out_ref[:, which] = jnp.where(head, turned, kept).reshape(per, width, ROWS)


def headed(rough, proj, edge, taps, grad_out):
    channels = proj.shape[-1]
    width = rough.shape[2]
    block = min(2048, channels)
    shape = (block // width, 2, width, ROWS)
    return pl.pallas_call(
        head_kernel,
        grid=(channels // block,),
        in_specs=[
            pl.BlockSpec(shape, lambda i: (i, 0, 0, 0)),
            pl.BlockSpec((3, 16, block), lambda i: (0, 0, i)),
            pl.BlockSpec((8, block), lambda i: (0, i)),
            pl.BlockSpec((3, 3, block), lambda i: (0, 0, i)),
            pl.BlockSpec((16, block), lambda i: (0, i)),
        ],
        out_specs=pl.BlockSpec(shape, lambda i: (i, 0, 0, 0)),
        out_shape=pltpu.HBM(rough.shape, jnp.bfloat16),
        compiler_params=params(32),
    )(rough, held(proj), edge, taps, held(grad_out))


def spectrum_kernel(filter_ref, fwd_a_ref, turn_ref, fwd_b_ref, out_ref):
    cos_w, sin_w = turn_ref[0], turn_ref[1]

    def one(ch, carry):
        high, low = split(filter_ref[ch])
        y = dot(fwd_a_ref[...], jnp.concatenate([high, high], axis=0))
        y += dot(fwd_a_ref[...], jnp.concatenate([low, low], axis=0))
        y_re, y_im = y[:ROWS], y[ROWS:]
        turned = jnp.concatenate(
            [y_re * cos_w - y_im * sin_w, y_re * sin_w + y_im * cos_w], axis=1
        )
        high, low = split(turned)
        out_ref[ch] = dot(high, fwd_b_ref[0]) + dot(high, fwd_b_ref[1]) + dot(low, fwd_b_ref[0])
        return carry

    lax.fori_loop(0, filter_ref.shape[0], one, 0, unroll=2)


def whole(shape):
    return pl.BlockSpec(shape, lambda *_: (0,) * len(shape))


def spectrum(filter_sq, tab):
    width = filter_sq.shape[0]
    block = min(8, width)
    return pl.pallas_call(
        spectrum_kernel,
        grid=(width // block,),
        in_specs=[
            pl.BlockSpec((block, ROWS, ROWS), lambda i: (i, 0, 0)),
            whole((2 * ROWS, 2 * ROWS)),
            whole((2, ROWS, ROWS)),
            whole((2, 2 * ROWS, 2 * ROWS)),
        ],
        out_specs=pl.BlockSpec((block, ROWS, 2 * ROWS), lambda i: (i, 0, 0)),
        out_shape=pltpu.HBM((width, ROWS, 2 * ROWS), jnp.float32),
        compiler_params=params(32),
        cost_estimate=pl.CostEstimate(
            flops=width * 5 * 2 * (2 * ROWS) ** 3, bytes_accessed=width * 3 * 4 * ROWS**2,
            transcendentals=0,
        ),
    )(filter_sq, tab["fwd_a"], tab["turn"], tab["fwd_b"])


def apply_right(rows, table_ref):
    total = dot(rows, table_ref[0])
    for term in range(1, table_ref.shape[0]):
        total += dot(rows, table_ref[term])
    return total


def apply_left(table_ref, columns):
    total = dot(table_ref[0], columns)
    for term in range(1, table_ref.shape[0]):
        total += dot(table_ref[term], columns)
    return total


def side(left, right):
    return jnp.concatenate([left.astype(jnp.bfloat16), right.astype(jnp.bfloat16)], axis=1)


def turned_back(spectra, inv_b_ref, inv_a_ref, cos_w, sin_w):
    v = apply_right(spectra, inv_b_ref)
    parts_re, parts_im = [], []
    for at in range(spectra.shape[0] // ROWS):
        v_re, v_im = halves(v[at * ROWS : (at + 1) * ROWS])
        parts_re.append((v_re * cos_w + v_im * sin_w).astype(jnp.bfloat16))
        parts_im.append((v_im * cos_w - v_re * sin_w).astype(jnp.bfloat16))
    parts = [jnp.concatenate(parts_re, axis=1), jnp.concatenate(parts_im, axis=1)]
    return apply_left(inv_a_ref, jnp.concatenate(parts, axis=0))


def conv_kernel(
    in_ref, spec_ref, fwd_a_ref, turn_ref, fwd_b_ref, inv_b_ref, inv_a_ref,
    out_ref, lag_ref, rows_ref, outs_ref, *, group,
):
    block = in_ref.shape[2]
    part = pl.program_id(1)

    @pl.when(part == 0)
    def _():
        for at in range(2):
            rows_ref[at] = in_ref[:, at].astype(jnp.float32).reshape(ROWS * block, ROWS)

    cos_w, sin_w = turn_ref[0], turn_ref[1]

    def some():
        chans = [part * group + at for at in range(group)]
        places = [(at, pl.ds(ch, ROWS, stride=block)) for ch in chans for at in range(2)]
        rows = [rows_ref[at, strided, :].astype(jnp.bfloat16) for at, strided in places]
        columns = jnp.concatenate(rows, axis=1)
        y = dot(fwd_a_ref[...], jnp.concatenate([columns, columns], axis=0))
        turned = []
        for at in range(2 * group):
            y_re = y[:ROWS, at * ROWS : (at + 1) * ROWS]
            y_im = y[ROWS:, at * ROWS : (at + 1) * ROWS]
            turned.append(side(y_re * cos_w - y_im * sin_w, y_re * sin_w + y_im * cos_w))
        z = apply_right(jnp.concatenate(turned, axis=0), fwd_b_ref)
        products = []
        for at in range(group):
            x_re, x_im = halves(z[2 * at * ROWS : (2 * at + 1) * ROWS])
            g_re, g_im = halves(z[(2 * at + 1) * ROWS : (2 * at + 2) * ROWS])
            h_re, h_im = halves(spec_ref[at])
            lag_ref[at] = side(g_re * x_re + g_im * x_im, g_im * x_re - g_re * x_im)
            products.append(side(x_re * h_re - x_im * h_im, x_re * h_im + x_im * h_re))
            products.append(side(h_re * g_re + h_im * g_im, h_re * g_im - h_im * g_re))
        res = turned_back(jnp.concatenate(products, axis=0), inv_b_ref, inv_a_ref, cos_w, sin_w)
        for column, (at, strided) in enumerate(places):
            outs_ref[at, strided, :] = res[:, column * ROWS : (column + 1) * ROWS]

    some()

    @pl.when(part == pl.num_programs(1) - 1)
    def _():
        for at in range(2):
            out_ref[:, at] = outs_ref[at].astype(jnp.bfloat16).reshape(ROWS, block, ROWS)


def convolve(received, spec, tab, group=8, block=16):
    width = received.shape[2]
    names = ("fwd_a", "turn", "fwd_b_high", "inv_b_high", "inv_a_high")
    return pl.pallas_call(
        functools.partial(conv_kernel, group=group),
        grid=(width // block, block // group),
        in_specs=[
            pl.BlockSpec((ROWS, 2, block, ROWS), lambda i, j: (0, 0, i, 0)),
            pl.BlockSpec((group, ROWS, 2 * ROWS), lambda i, j: (i * (block // group) + j, 0, 0)),
        ]
        + [whole(tab[name].shape) for name in names],
        out_specs=[
            pl.BlockSpec((ROWS, 2, block, ROWS), lambda i, j: (0, 0, i, 0)),
            pl.BlockSpec((group, ROWS, 2 * ROWS), lambda i, j: (i * (block // group) + j, 0, 0)),
        ],
        out_shape=[
            pltpu.HBM((ROWS, 2, width, ROWS), jnp.bfloat16),
            pltpu.HBM((width, ROWS, 2 * ROWS), jnp.bfloat16),
        ],
        scratch_shapes=[pltpu.VMEM((2, ROWS * block, ROWS), jnp.float32)] * 2,
        compiler_params=params(40),
    )(received, held(spec), *(tab[name] for name in names))


def lag_kernel(products_ref, turn_ref, inv_b_ref, inv_a_ref, out_ref):
    count = products_ref.shape[0]
    products = products_ref[...].reshape(count * ROWS, 2 * ROWS)
    res = turned_back(products, inv_b_ref, inv_a_ref, turn_ref[0], turn_ref[1])
    for ch in range(count):
        out_ref[ch] = res[:, ch * ROWS : (ch + 1) * ROWS]


def lags(products, tab):
    width = products.shape[0]
    block = min(8, width)
    names = ("turn", "inv_b", "inv_a")
    return pl.pallas_call(
        lag_kernel,
        grid=(width // block,),
        in_specs=[pl.BlockSpec((block, ROWS, 2 * ROWS), lambda i: (i, 0, 0))]
        + [whole(tab[name].shape) for name in names],
        out_specs=pl.BlockSpec((block, ROWS, ROWS), lambda i: (i, 0, 0)),
        out_shape=jax.ShapeDtypeStruct((width, ROWS, ROWS), jnp.float32),
        compiler_params=params(32),
        cost_estimate=pl.CostEstimate(
            flops=width * 4 * 2 * (2 * ROWS) ** 3, bytes_accessed=width * 8 * ROWS**2,
            transcendentals=0,
        ),
    )(products, *(tab[name] for name in names))


def fill_turned(turned_ref, ret_ref):
    block = turned_ref.shape[2]
    for at in range(2):
        turned_ref[at] = ret_ref[:, at].reshape(block, ROWS).T.astype(jnp.float32)


def grads_at(turned_ref, taps_ref, grad_ref, row, lanes, keys, values):
    rows = pl.ds(row, STEP)
    conv, corr = turned_ref[0, rows, lanes], turned_ref[1, rows, lanes]
    key = filtered(taps_ref, 1, lanes, keys)
    value = filtered(taps_ref, 2, lanes, values)
    return (grad_ref[rows, lanes].astype(jnp.float32) * conv, corr * value, corr * key)


def sums_kernel(
    ret_ref, proj_ref, edge_ref, taps_ref, grad_ref, sums_ref, first_ref, ext_ref, turned_ref
):
    fill_ext(ext_ref, proj_ref, edge_ref)
    fill_turned(turned_ref, ret_ref)
    first_ref[...] = jnp.zeros_like(first_ref)
    sums_ref[...] = jnp.zeros_like(sums_ref)
    for at, lanes in enumerate(lanes_of(grad_ref.shape[1])):
        sums = [jnp.zeros((8, ROWS), jnp.float32)] * 9
        for row in range(0, ROWS, STEP):
            shifted = [inputs_at(ext_ref, stream, row, lanes) for stream in range(3)]
            grads = grads_at(turned_ref, taps_ref, grad_ref, row, lanes, shifted[1], shifted[2])
            for stream in range(3):
                for tap in range(3):
                    terms = (grads[stream] * shifted[stream][tap]).reshape(STEP // 8, 8, ROWS)
                    sums[3 * stream + tap] = sums[3 * stream + tap] + jnp.sum(terms, axis=0)
                if row == 0:
                    first_ref[pl.ds(2 * stream, 2), lanes] = grads[stream][:2]
        for which in range(9):
            sums_ref[which, pl.ds(at, 1)] = jnp.sum(sums[which], axis=0, keepdims=True)


def local_specs(block, width):
    return [
        pl.BlockSpec((block // width, 2, width, ROWS), lambda i: (i, 0, 0, 0)),
        pl.BlockSpec((3, ROWS, block), lambda i: (0, 0, i)),
        pl.BlockSpec((8, block), lambda i: (0, i)),
        pl.BlockSpec((3, 3, block), lambda i: (0, 0, i)),
        pl.BlockSpec((ROWS, block), lambda i: (0, i)),
    ]


def tap_sums(returned, proj, edge, taps, grad_out):
    channels = proj.shape[-1]
    block = min(1024, channels)
    return pl.pallas_call(
        sums_kernel,
        grid=(channels // block,),
        in_specs=local_specs(block, returned.shape[2]),
        out_specs=[
            pl.BlockSpec((16, block // ROWS, ROWS), lambda i: (0, i, 0)),
            pl.BlockSpec((8, block), lambda i: (0, i)),
        ],
        out_shape=[
            jax.ShapeDtypeStruct((16, channels // ROWS, ROWS), jnp.float32),
            jax.ShapeDtypeStruct((8, channels), jnp.float32),
        ],
        scratch_shapes=[
            pltpu.VMEM((3, ROWS + 8, block), jnp.float32),
            pltpu.VMEM((2, ROWS, block), jnp.float32),
        ],
        compiler_params=params(40),
    )(returned, held(proj), edge, taps, held(grad_out))


def grads_kernel(
    ret_ref, proj_ref, edge_ref, taps_ref, grad_ref, later_ref,
    out_ref, ext_ref, turned_ref, grads_ref,
):
    fill_ext(ext_ref, proj_ref, edge_ref)
    fill_turned(turned_ref, ret_ref)
    for stream in range(3):
        grads_ref[stream, pl.ds(ROWS, 2), :] = later_ref[pl.ds(2 * stream, 2), :]
    for lanes in lanes_of(grad_ref.shape[1]):
        for row in range(0, ROWS, STEP):
            shifted = [inputs_at(ext_ref, stream, row, lanes) for stream in (1, 2)]
            grads = grads_at(turned_ref, taps_ref, grad_ref, row, lanes, *shifted)
            for stream in range(3):
                grads_ref[stream, pl.ds(row, STEP), lanes] = grads[stream]
        for stream in range(3):
            for row in range(0, ROWS, STEP):
                ahead = [grads_ref[stream, pl.ds(row + tap, STEP), lanes] for tap in range(3)]
                total = filtered(taps_ref, stream, lanes, ahead)
                out_ref[stream, pl.ds(row, STEP), lanes] = total.astype(jnp.bfloat16)


def stream_grads(returned, proj, edge, taps, grad_out, later):
    channels = proj.shape[-1]
    block = min(1024, channels)
    return pl.pallas_call(
        grads_kernel,
        grid=(channels // block,),
        in_specs=local_specs(block, returned.shape[2])
        + [pl.BlockSpec((8, block), lambda i: (0, i))],
        out_specs=pl.BlockSpec((3, ROWS, block), lambda i: (0, 0, i)),
        out_shape=jax.ShapeDtypeStruct((3, ROWS, channels), jnp.bfloat16),
        scratch_shapes=[
            pltpu.VMEM((3, ROWS + 8, block), jnp.float32),
            pltpu.VMEM((2, ROWS, block), jnp.float32),
            pltpu.VMEM((3, ROWS + 8, block), jnp.float32),
        ],
        compiler_params=params(40),
        cost_estimate=pl.CostEstimate(
            flops=60 * ROWS * channels, bytes_accessed=18 * ROWS * channels, transcendentals=0
        ),
    )(returned, held(proj), edge, taps, held(grad_out), later)


def passed_along(value, steps):
    count = lax.axis_size("ctx")
    initial, last = (max(0, -steps), min(count, count - steps))
    return lax.ppermute(value, "ctx", [(source, source + steps) for source in range(initial, last)])


def exchanged(value, axes):
    return lax.all_to_all(value, axes, split_axis=0, concat_axis=0, tiled=True)


def sum_everywhere(sums, beside):
    channels = sums.shape[1] * ROWS
    devices = lax.axis_size("dp") * lax.axis_size("ctx")
    pieces = sums.reshape(devices, 2, ROWS)
    own = jnp.sum(exchanged(pieces, ("dp", "ctx")), axis=0)
    own, beside = lax.optimization_barrier((own.astype(jnp.bfloat16), beside))
    spread = exchanged(jnp.broadcast_to(own[None], pieces.shape), ("dp", "ctx"))
    return spread.reshape(16, channels)[:9].reshape(3, 3, channels).astype(jnp.float32), beside


def local(projected, short_taps, long_filter, grad_out):
    tab = tables()
    proj = projected[:, 0]
    grad_rows = grad_out[0]
    width = long_filter.shape[0]
    edge = passed_along(edges(proj), 1)
    rough = gates(proj, short_taps, grad_rows, width)
    sent = headed(rough, proj, edge, short_taps, grad_rows)
    received = exchanged(sent, "ctx")
    spec = spectrum(long_filter.reshape(width, ROWS, ROWS), tab)
    results, products = convolve(received, spec, tab)
    returned = exchanged(results, "ctx")
    lag = lags(products, tab)
    second = lax.axis_index("dp") == 1
    lower, upper = lag[:, : ROWS // 2], lag[:, ROWS // 2 :]
    other = lax.ppermute(
        jnp.where(second, lower, upper).astype(jnp.bfloat16), "dp", [(0, 1), (1, 0)]
    )
    lag_sum = jnp.where(second, upper, lower) + other.astype(jnp.float32)
    grad_filter = lag_sum.reshape(width, ROWS // 2 * ROWS)
    late_edge, grad_filter = lax.optimization_barrier((edge, grad_filter))
    sums, first = tap_sums(returned, proj, late_edge, short_taps, grad_rows)
    grad_taps, later = sum_everywhere(sums, passed_along(first, -1))
    grad_in = stream_grads(returned, proj, edge, short_taps, grad_rows, later)
    return (grad_in[:, None], grad_taps, grad_filter)


def solution(mesh):
    return jax.shard_map(
        local,
        mesh=mesh,
        in_specs=(P(None, "dp", "ctx", None), P(), P("ctx", None), P("dp", "ctx", None)),
        out_specs=(P(None, "dp", "ctx", None), P(), P("ctx", "dp")),
        check_vma=False,
    )
```

```python
import functools
import math

import jax
import jax.numpy as jnp
import numpy as np
from jax import lax
from jax.experimental import pallas as pl
from jax.experimental.pallas import tpu as pltpu
from jax.sharding import PartitionSpec as P

ROWS = 128
MIB = 2**20


def rounded(table):
    high = table.astype(jnp.bfloat16)
    low = (table - high.astype(np.float64)).astype(jnp.bfloat16)
    return high, low


@functools.cache
def tables():
    idx = np.arange(ROWS, dtype=np.float64)
    quarter = idx + 0.25
    ang_a = 2.0 * math.pi * np.outer(quarter, idx) / ROWS
    fwd_a = np.concatenate([np.cos(ang_a), -np.sin(ang_a)], axis=0)
    inv_a = np.concatenate([np.cos(ang_a.T), -np.sin(ang_a.T)], axis=1) / ROWS**2
    ang_w = 2.0 * math.pi * np.outer(quarter, idx) / ROWS**2
    turn = np.stack([np.cos(ang_w), -np.sin(ang_w)]).astype(np.float32)
    ang_b = 2.0 * math.pi * (np.outer(idx, idx) % ROWS) / ROWS
    cos_b, sin_b = np.cos(ang_b), np.sin(ang_b)
    fwd_b = np.block([[cos_b, -sin_b], [sin_b, cos_b]])
    inv_b = np.block([[cos_b, sin_b], [-sin_b, cos_b]])
    return {
        "fwd_a": np.concatenate(rounded(fwd_a), axis=1),
        "turn": turn,
        "fwd_b": np.stack(rounded(fwd_b)),
        "fwd_b_high": np.stack(rounded(fwd_b)[:1]),
        "inv_b": np.stack(rounded(inv_b)),
        "inv_b_high": np.stack(rounded(inv_b)[:1]),
        "inv_a": np.stack(rounded(inv_a)),
        "inv_a_high": np.stack(rounded(inv_a)[:1]),
    }


def dot(lhs, rhs):
    return lax.dot_general(lhs, rhs, (((1,), (0,)), ((), ())), preferred_element_type=jnp.float32)


def split(value):
    high = value.astype(jnp.bfloat16)
    return high, (value - high.astype(jnp.float32)).astype(jnp.bfloat16)


def halves(value):
    return value[:, :ROWS], value[:, ROWS:]


def held(value):
    return pltpu.with_memory_space_constraint(value, pltpu.HBM)


def params(mib=48):
    return pltpu.CompilerParams(vmem_limit_bytes=mib * MIB)


def fill_ext(ext_ref, proj_ref, edge_ref):
    for stream in range(3):
        ext_ref[stream, pl.ds(8, ROWS), :] = proj_ref[stream].astype(jnp.float32)
        ext_ref[stream, pl.ds(6, 2), :] = edge_ref[pl.ds(2 * stream, 2), :]


def edge_kernel(proj_ref, out_ref):
    out_ref[...] = jnp.zeros_like(out_ref)
    for stream in range(3):
        tail = proj_ref[stream].astype(jnp.float32)
        out_ref[pl.ds(2 * stream, 2), :] = tail[14:16, :]


def edges(proj):
    channels = proj.shape[-1]
    return pl.pallas_call(
        edge_kernel,
        grid=(1,),
        in_specs=[pl.BlockSpec((3, 16, channels), lambda i: (0, ROWS // 16 - 1, 0))],
        out_specs=pl.BlockSpec((8, channels), lambda i: (0, 0)),
        out_shape=jax.ShapeDtypeStruct((8, channels), jnp.float32),
        compiler_params=params(16),
    )(held(proj))


STEP = 32


def lanes_of(width):
    return [pl.ds(at, ROWS) for at in range(0, width, ROWS)]


def inputs_at(ext_ref, stream, row, lanes):
    rows = ext_ref[stream, pl.ds(row, STEP + 8), lanes]
    return [rows[8:]] + [pltpu.roll(rows, tap, 0)[8:] for tap in (1, 2)]


def filtered(taps_ref, stream, lanes, shifted):
    rows = taps_ref[stream, :, lanes]
    return sum(rows[tap : tap + 1] * shifted[tap] for tap in range(3))


def gate_kernel(proj_ref, taps_ref, grad_ref, out_ref, ext_ref):
    for stream in range(3):
        ext_ref[stream, pl.ds(8, ROWS), :] = proj_ref[stream].astype(jnp.float32)
        ext_ref[stream, pl.ds(0, 8), :] = jnp.zeros((8, grad_ref.shape[1]), jnp.float32)
    width = out_ref.shape[2]
    per = ROWS // width
    for at, lanes in enumerate(lanes_of(grad_ref.shape[1])):
        gated, grad_gate = [], []
        for row in range(0, ROWS, STEP):
            query, key, value = (
                filtered(taps_ref, stream, lanes, inputs_at(ext_ref, stream, row, lanes))
                for stream in range(3)
            )
            grad = grad_ref[pl.ds(row, STEP), lanes].astype(jnp.float32)
            gated.append((key * value).astype(jnp.bfloat16))
            grad_gate.append((grad * query).astype(jnp.bfloat16))
        for which, parts in enumerate((gated, grad_gate)):
            turned = jnp.concatenate(parts, axis=0).T
            out_ref[pl.ds(at * per, per), which] = turned.reshape(per, width, ROWS)


def gates(proj, taps, grad_out, width):
    channels = proj.shape[-1]
    block = min(2048, channels)
    return pl.pallas_call(
        gate_kernel,
        grid=(channels // block,),
        in_specs=[
            pl.BlockSpec((3, ROWS, block), lambda i: (0, 0, i)),
            pl.BlockSpec((3, 3, block), lambda i: (0, 0, i)),
            pl.BlockSpec((ROWS, block), lambda i: (0, i)),
        ],
        out_specs=pl.BlockSpec((block // width, 2, width, ROWS), lambda i: (i, 0, 0, 0)),
        out_shape=jax.ShapeDtypeStruct((channels // width, 2, width, ROWS), jnp.bfloat16),
        scratch_shapes=[pltpu.VMEM((3, ROWS + 8, block), jnp.float32)],
        compiler_params=params(32),
        cost_estimate=pl.CostEstimate(
            flops=40 * ROWS * channels, bytes_accessed=12 * ROWS * channels, transcendentals=0
        ),
    )(held(proj), taps, held(grad_out))


def head_kernel(rough_ref, proj_ref, edge_ref, taps_ref, grad_ref, out_ref):
    per, _, width, _ = out_ref.shape
    block = per * width
    features = []
    for stream in range(3):
        before = edge_ref[pl.ds(2 * stream, 2), :]
        rows = jnp.concatenate([before, proj_ref[stream].astype(jnp.float32)[:2]], axis=0)
        features.append(
            sum(taps_ref[stream, pl.ds(tap, 1), :] * rows[2 - tap : 4 - tap] for tap in range(3))
        )
    query, key, value = features
    grad = grad_ref[...].astype(jnp.float32)[:2]
    below = jnp.zeros((ROWS - 2, block), jnp.float32)
    head = lax.broadcasted_iota(jnp.int32, (block, ROWS), 1) < 2
    for which, rows in enumerate((key * value, grad * query)):
        turned = jnp.concatenate([rows, below], axis=0).astype(jnp.bfloat16).T
        kept = rough_ref[:, which].reshape(block, ROWS)
        out_ref[:, which] = jnp.where(head, turned, kept).reshape(per, width, ROWS)


def headed(rough, proj, edge, taps, grad_out):
    channels = proj.shape[-1]
    width = rough.shape[2]
    block = min(2048, channels)
    shape = (block // width, 2, width, ROWS)
    return pl.pallas_call(
        head_kernel,
        grid=(channels // block,),
        in_specs=[
            pl.BlockSpec(shape, lambda i: (i, 0, 0, 0)),
            pl.BlockSpec((3, 16, block), lambda i: (0, 0, i)),
            pl.BlockSpec((8, block), lambda i: (0, i)),
            pl.BlockSpec((3, 3, block), lambda i: (0, 0, i)),
            pl.BlockSpec((16, block), lambda i: (0, i)),
        ],
        out_specs=pl.BlockSpec(shape, lambda i: (i, 0, 0, 0)),
        out_shape=pltpu.HBM(rough.shape, jnp.bfloat16),
        compiler_params=params(32),
    )(rough, held(proj), edge, taps, held(grad_out))


def spectrum_kernel(filter_ref, fwd_a_ref, turn_ref, fwd_b_ref, out_ref):
    cos_w, sin_w = turn_ref[0], turn_ref[1]

    def one(ch, carry):
        high, low = split(filter_ref[ch])
        y = dot(fwd_a_ref[...], jnp.concatenate([high, high], axis=0))
        y += dot(fwd_a_ref[...], jnp.concatenate([low, low], axis=0))
        y_re, y_im = y[:ROWS], y[ROWS:]
        turned = jnp.concatenate(
            [y_re * cos_w - y_im * sin_w, y_re * sin_w + y_im * cos_w], axis=1
        )
        high, low = split(turned)
        out_ref[ch] = dot(high, fwd_b_ref[0]) + dot(high, fwd_b_ref[1]) + dot(low, fwd_b_ref[0])
        return carry

    lax.fori_loop(0, filter_ref.shape[0], one, 0, unroll=2)


def whole(shape):
    return pl.BlockSpec(shape, lambda *_: (0,) * len(shape))


def spectrum(filter_sq, tab):
    width = filter_sq.shape[0]
    block = min(8, width)
    return pl.pallas_call(
        spectrum_kernel,
        grid=(width // block,),
        in_specs=[
            pl.BlockSpec((block, ROWS, ROWS), lambda i: (i, 0, 0)),
            whole((2 * ROWS, 2 * ROWS)),
            whole((2, ROWS, ROWS)),
            whole((2, 2 * ROWS, 2 * ROWS)),
        ],
        out_specs=pl.BlockSpec((block, ROWS, 2 * ROWS), lambda i: (i, 0, 0)),
        out_shape=pltpu.HBM((width, ROWS, 2 * ROWS), jnp.float32),
        compiler_params=params(32),
        cost_estimate=pl.CostEstimate(
            flops=width * 5 * 2 * (2 * ROWS) ** 3, bytes_accessed=width * 3 * 4 * ROWS**2,
            transcendentals=0,
        ),
    )(filter_sq, tab["fwd_a"], tab["turn"], tab["fwd_b"])


def apply_right(rows, table_ref):
    total = dot(rows, table_ref[0])
    for term in range(1, table_ref.shape[0]):
        total += dot(rows, table_ref[term])
    return total


def apply_left(table_ref, columns):
    total = dot(table_ref[0], columns)
    for term in range(1, table_ref.shape[0]):
        total += dot(table_ref[term], columns)
    return total


def side(left, right):
    return jnp.concatenate([left.astype(jnp.bfloat16), right.astype(jnp.bfloat16)], axis=1)


def turned_back(spectra, inv_b_ref, inv_a_ref, cos_w, sin_w):
    v = apply_right(spectra, inv_b_ref)
    parts_re, parts_im = [], []
    for at in range(spectra.shape[0] // ROWS):
        v_re, v_im = halves(v[at * ROWS : (at + 1) * ROWS])
        parts_re.append((v_re * cos_w + v_im * sin_w).astype(jnp.bfloat16))
        parts_im.append((v_im * cos_w - v_re * sin_w).astype(jnp.bfloat16))
    parts = [jnp.concatenate(parts_re, axis=1), jnp.concatenate(parts_im, axis=1)]
    return apply_left(inv_a_ref, jnp.concatenate(parts, axis=0))


def conv_kernel(
    in_ref, spec_ref, fwd_a_ref, turn_ref, fwd_b_ref, inv_b_ref, inv_a_ref,
    out_ref, lag_ref, rows_ref, outs_ref, *, group,
):
    block = out_ref.shape[2]
    part = pl.program_id(1)
    here = pl.ds(pl.multiple_of(pl.program_id(0) * block, block), block)

    @pl.when(part == 0)
    def _():
        for at in range(2):
            rows_ref[at] = in_ref[:, at, here].astype(jnp.float32).reshape(ROWS * block, ROWS)

    cos_w, sin_w = turn_ref[0], turn_ref[1]

    def some():
        chans = [part * group + at for at in range(group)]
        places = [(at, pl.ds(ch, ROWS, stride=block)) for ch in chans for at in range(2)]
        rows = [rows_ref[at, strided, :].astype(jnp.bfloat16) for at, strided in places]
        columns = jnp.concatenate(rows, axis=1)
        y = dot(fwd_a_ref[...], jnp.concatenate([columns, columns], axis=0))
        turned = []
        for at in range(2 * group):
            y_re = y[:ROWS, at * ROWS : (at + 1) * ROWS]
            y_im = y[ROWS:, at * ROWS : (at + 1) * ROWS]
            turned.append(side(y_re * cos_w - y_im * sin_w, y_re * sin_w + y_im * cos_w))
        z = apply_right(jnp.concatenate(turned, axis=0), fwd_b_ref)
        products = []
        for at in range(group):
            x_re, x_im = halves(z[2 * at * ROWS : (2 * at + 1) * ROWS])
            g_re, g_im = halves(z[(2 * at + 1) * ROWS : (2 * at + 2) * ROWS])
            h_re, h_im = halves(spec_ref[at])
            lag_ref[at] = side(g_re * x_re + g_im * x_im, g_im * x_re - g_re * x_im)
            products.append(side(x_re * h_re - x_im * h_im, x_re * h_im + x_im * h_re))
            products.append(side(h_re * g_re + h_im * g_im, h_re * g_im - h_im * g_re))
        res = turned_back(jnp.concatenate(products, axis=0), inv_b_ref, inv_a_ref, cos_w, sin_w)
        for column, (at, strided) in enumerate(places):
            outs_ref[at, strided, :] = res[:, column * ROWS : (column + 1) * ROWS]

    some()

    @pl.when(part == pl.num_programs(1) - 1)
    def _():
        for at in range(2):
            out_ref[:, at] = outs_ref[at].astype(jnp.bfloat16).reshape(ROWS, block, ROWS)


def convolve(received, spec, tab, group=8, block=16):
    width = received.shape[2]
    names = ("fwd_a", "turn", "fwd_b_high", "inv_b_high", "inv_a_high")
    return pl.pallas_call(
        functools.partial(conv_kernel, group=group),
        grid=(width // block, block // group),
        in_specs=[
            pl.BlockSpec(memory_space=pltpu.VMEM),
            pl.BlockSpec((group, ROWS, 2 * ROWS), lambda i, j: (i * (block // group) + j, 0, 0)),
        ]
        + [whole(tab[name].shape) for name in names],
        out_specs=[
            pl.BlockSpec((ROWS, 2, block, ROWS), lambda i, j: (0, 0, i, 0)),
            pl.BlockSpec((group, ROWS, 2 * ROWS), lambda i, j: (i * (block // group) + j, 0, 0)),
        ],
        out_shape=[
            pltpu.HBM((ROWS, 2, width, ROWS), jnp.bfloat16),
            pltpu.HBM((width, ROWS, 2 * ROWS), jnp.bfloat16),
        ],
        scratch_shapes=[pltpu.VMEM((2, ROWS * block, ROWS), jnp.float32)] * 2,
        compiler_params=params(40),
    )(received, held(spec), *(tab[name] for name in names))


def lag_kernel(products_ref, turn_ref, inv_b_ref, inv_a_ref, out_ref):
    count = products_ref.shape[0]
    products = products_ref[...].reshape(count * ROWS, 2 * ROWS)
    res = turned_back(products, inv_b_ref, inv_a_ref, turn_ref[0], turn_ref[1])
    for ch in range(count):
        out_ref[ch] = res[:, ch * ROWS : (ch + 1) * ROWS]


def lags(products, tab):
    width = products.shape[0]
    block = min(8, width)
    names = ("turn", "inv_b", "inv_a")
    return pl.pallas_call(
        lag_kernel,
        grid=(width // block,),
        in_specs=[pl.BlockSpec((block, ROWS, 2 * ROWS), lambda i: (i, 0, 0))]
        + [whole(tab[name].shape) for name in names],
        out_specs=pl.BlockSpec((block, ROWS, ROWS), lambda i: (i, 0, 0)),
        out_shape=jax.ShapeDtypeStruct((width, ROWS, ROWS), jnp.float32),
        compiler_params=params(32),
        cost_estimate=pl.CostEstimate(
            flops=width * 4 * 2 * (2 * ROWS) ** 3, bytes_accessed=width * 8 * ROWS**2,
            transcendentals=0,
        ),
    )(products, *(tab[name] for name in names))


def fill_turned(turned_ref, ret_ref):
    block = turned_ref.shape[2]
    for at in range(2):
        turned_ref[at] = ret_ref[:, at].reshape(block, ROWS).T.astype(jnp.float32)


def grads_at(turned_ref, taps_ref, grad_ref, row, lanes, keys, values):
    rows = pl.ds(row, STEP)
    conv, corr = turned_ref[0, rows, lanes], turned_ref[1, rows, lanes]
    key = filtered(taps_ref, 1, lanes, keys)
    value = filtered(taps_ref, 2, lanes, values)
    return (grad_ref[rows, lanes].astype(jnp.float32) * conv, corr * value, corr * key)


def sums_kernel(
    ret_ref, proj_ref, edge_ref, taps_ref, grad_ref, sums_ref, first_ref, ext_ref, turned_ref
):
    block = grad_ref.shape[1]
    channels = pl.ds(pl.multiple_of(pl.program_id(0) * block, block), block)
    fill_ext(ext_ref, proj_ref.at[:, :, channels], edge_ref)
    fill_turned(turned_ref, ret_ref)
    first_ref[...] = jnp.zeros_like(first_ref)
    sums_ref[...] = jnp.zeros_like(sums_ref)
    for at, lanes in enumerate(lanes_of(grad_ref.shape[1])):
        sums = [jnp.zeros((8, ROWS), jnp.float32)] * 9
        for row in range(0, ROWS, STEP):
            shifted = [inputs_at(ext_ref, stream, row, lanes) for stream in range(3)]
            grads = grads_at(turned_ref, taps_ref, grad_ref, row, lanes, shifted[1], shifted[2])
            for stream in range(3):
                for tap in range(3):
                    terms = (grads[stream] * shifted[stream][tap]).reshape(STEP // 8, 8, ROWS)
                    sums[3 * stream + tap] = sums[3 * stream + tap] + jnp.sum(terms, axis=0)
                if row == 0:
                    first_ref[pl.ds(2 * stream, 2), lanes] = grads[stream][:2]
        for which in range(9):
            sums_ref[which, pl.ds(at, 1)] = jnp.sum(sums[which], axis=0, keepdims=True)


def local_specs(block, width):
    return [
        pl.BlockSpec((block // width, 2, width, ROWS), lambda i: (i, 0, 0, 0)),
        pl.BlockSpec((3, ROWS, block), lambda i: (0, 0, i)),
        pl.BlockSpec((8, block), lambda i: (0, i)),
        pl.BlockSpec((3, 3, block), lambda i: (0, 0, i)),
        pl.BlockSpec((ROWS, block), lambda i: (0, i)),
    ]


def tap_sums(returned, proj, edge, taps, grad_out):
    channels = proj.shape[-1]
    block = min(1024, channels)
    specs = local_specs(block, returned.shape[2])
    specs[1] = pl.BlockSpec(memory_space=pltpu.VMEM)
    return pl.pallas_call(
        sums_kernel,
        grid=(channels // block,),
        in_specs=specs,
        out_specs=[
            pl.BlockSpec((16, block // ROWS, ROWS), lambda i: (0, i, 0)),
            pl.BlockSpec((8, block), lambda i: (0, i)),
        ],
        out_shape=[
            pltpu.HBM((16, channels // ROWS, ROWS), jnp.float32),
            pltpu.HBM((8, channels), jnp.float32),
        ],
        scratch_shapes=[
            pltpu.VMEM((3, ROWS + 8, block), jnp.float32),
            pltpu.VMEM((2, ROWS, block), jnp.float32),
        ],
        compiler_params=params(40),
    )(returned, proj, edge, taps, held(grad_out))


def grads_kernel(
    ret_ref, proj_ref, edge_ref, taps_ref, grad_ref, later_ref,
    out_ref, ext_ref, turned_ref, grads_ref,
):
    fill_ext(ext_ref, proj_ref, edge_ref)
    fill_turned(turned_ref, ret_ref)
    for stream in range(3):
        grads_ref[stream, pl.ds(ROWS, 2), :] = later_ref[pl.ds(2 * stream, 2), :]
    for lanes in lanes_of(grad_ref.shape[1]):
        for row in range(0, ROWS, STEP):
            shifted = [inputs_at(ext_ref, stream, row, lanes) for stream in (1, 2)]
            grads = grads_at(turned_ref, taps_ref, grad_ref, row, lanes, *shifted)
            for stream in range(3):
                grads_ref[stream, pl.ds(row, STEP), lanes] = grads[stream]
        for stream in range(3):
            for row in range(0, ROWS, STEP):
                ahead = [grads_ref[stream, pl.ds(row + tap, STEP), lanes] for tap in range(3)]
                total = filtered(taps_ref, stream, lanes, ahead)
                out_ref[stream, pl.ds(row, STEP), lanes] = total.astype(jnp.bfloat16)


def stream_grads(returned, proj, edge, taps, grad_out, later):
    channels = proj.shape[-1]
    block = min(1024, channels)
    return pl.pallas_call(
        grads_kernel,
        grid=(channels // block,),
        in_specs=local_specs(block, returned.shape[2])
        + [pl.BlockSpec((8, block), lambda i: (0, i))],
        out_specs=pl.BlockSpec((3, ROWS, block), lambda i: (0, 0, i)),
        out_shape=jax.ShapeDtypeStruct((3, ROWS, channels), jnp.bfloat16),
        scratch_shapes=[
            pltpu.VMEM((3, ROWS + 8, block), jnp.float32),
            pltpu.VMEM((2, ROWS, block), jnp.float32),
            pltpu.VMEM((3, ROWS + 8, block), jnp.float32),
        ],
        compiler_params=params(40),
        cost_estimate=pl.CostEstimate(
            flops=60 * ROWS * channels, bytes_accessed=18 * ROWS * channels, transcendentals=0
        ),
    )(returned, held(proj), edge, taps, held(grad_out), later)


def passed_along(value, steps):
    count = lax.axis_size("ctx")
    initial, last = (max(0, -steps), min(count, count - steps))
    return lax.ppermute(value, "ctx", [(source, source + steps) for source in range(initial, last)])


def exchanged(value, axes):
    return lax.all_to_all(value, axes, split_axis=0, concat_axis=0, tiled=True)


def sum_everywhere(sums, beside):
    channels = sums.shape[1] * ROWS
    devices = lax.axis_size("dp") * lax.axis_size("ctx")
    pieces = sums.reshape(devices, 2, ROWS)
    own = jnp.sum(exchanged(pieces, ("dp", "ctx")), axis=0)
    own, beside = lax.optimization_barrier((own.astype(jnp.bfloat16), beside))
    spread = exchanged(jnp.broadcast_to(own[None], pieces.shape), ("dp", "ctx"))
    return spread.reshape(16, channels)[:9].reshape(3, 3, channels).astype(jnp.float32), beside


def local(projected, short_taps, long_filter, grad_out):
    tab = tables()
    proj = projected[:, 0]
    grad_rows = grad_out[0]
    width = long_filter.shape[0]
    edge = passed_along(edges(proj), 1)
    rough = gates(proj, short_taps, grad_rows, width)
    sent = headed(rough, proj, edge, short_taps, grad_rows)
    received = exchanged(sent, "ctx")
    spec = spectrum(long_filter.reshape(width, ROWS, ROWS), tab)
    results, products = convolve(received, spec, tab)
    returned = exchanged(results, "ctx")
    lag = lags(products, tab)
    second = lax.axis_index("dp") == 1
    lower, upper = lag[:, : ROWS // 2], lag[:, ROWS // 2 :]
    other = lax.ppermute(
        jnp.where(second, lower, upper).astype(jnp.bfloat16), "dp", [(0, 1), (1, 0)]
    )
    lag_sum = jnp.where(second, upper, lower) + other.astype(jnp.float32)
    grad_filter = lag_sum.reshape(width, ROWS // 2 * ROWS)
    late_edge, grad_filter = lax.optimization_barrier((edge, grad_filter))
    sums, first = tap_sums(returned, proj, late_edge, short_taps, grad_rows)
    grad_taps, later = sum_everywhere(sums, passed_along(first, -1))
    grad_in = stream_grads(returned, proj, edge, short_taps, grad_rows, later)
    return (grad_in[:, None], grad_taps, grad_filter)


def solution(mesh):
    return jax.shard_map(
        local,
        mesh=mesh,
        in_specs=(P(None, "dp", "ctx", None), P(), P("ctx", None), P("dp", "ctx", None)),
        out_specs=(P(None, "dp", "ctx", None), P(), P("ctx", "dp")),
        check_vma=False,
    )
```

```python
import functools
import math

import jax
import jax.numpy as jnp
import numpy as np
from jax import lax
from jax.experimental import pallas as pl
from jax.experimental.pallas import tpu as pltpu
from jax.sharding import PartitionSpec as P

ROWS = 128
MIB = 2**20


def rounded(table):
    high = table.astype(jnp.bfloat16)
    low = (table - high.astype(np.float64)).astype(jnp.bfloat16)
    return high, low


@functools.cache
def tables():
    idx = np.arange(ROWS, dtype=np.float64)
    quarter = idx + 0.25
    ang_a = 2.0 * math.pi * np.outer(quarter, idx) / ROWS
    fwd_a = np.concatenate([np.cos(ang_a), -np.sin(ang_a)], axis=0)
    inv_a = np.concatenate([np.cos(ang_a.T), -np.sin(ang_a.T)], axis=1) / ROWS**2
    ang_w = 2.0 * math.pi * np.outer(quarter, idx) / ROWS**2
    turn = np.stack([np.cos(ang_w), -np.sin(ang_w)]).astype(np.float32)
    ang_b = 2.0 * math.pi * (np.outer(idx, idx) % ROWS) / ROWS
    cos_b, sin_b = np.cos(ang_b), np.sin(ang_b)
    fwd_b = np.block([[cos_b, -sin_b], [sin_b, cos_b]])
    inv_b = np.block([[cos_b, sin_b], [-sin_b, cos_b]])
    return {
        "fwd_a": np.concatenate(rounded(fwd_a), axis=1),
        "turn": turn,
        "fwd_b": np.stack(rounded(fwd_b)),
        "fwd_b_high": np.stack(rounded(fwd_b)[:1]),
        "inv_b": np.stack(rounded(inv_b)),
        "inv_b_high": np.stack(rounded(inv_b)[:1]),
        "inv_a": np.stack(rounded(inv_a)),
        "inv_a_high": np.stack(rounded(inv_a)[:1]),
    }


def dot(lhs, rhs):
    return lax.dot_general(lhs, rhs, (((1,), (0,)), ((), ())), preferred_element_type=jnp.float32)


def split(value):
    high = value.astype(jnp.bfloat16)
    return high, (value - high.astype(jnp.float32)).astype(jnp.bfloat16)


def halves(value):
    return value[:, :ROWS], value[:, ROWS:]


def held(value):
    return pltpu.with_memory_space_constraint(value, pltpu.HBM)


def params(mib=48):
    return pltpu.CompilerParams(vmem_limit_bytes=mib * MIB)


def fill_ext(ext_ref, proj_ref, edge_ref):
    for stream in range(3):
        ext_ref[stream, pl.ds(8, ROWS), :] = proj_ref[stream].astype(jnp.float32)
        ext_ref[stream, pl.ds(6, 2), :] = edge_ref[pl.ds(2 * stream, 2), :]


def edge_kernel(proj_ref, out_ref):
    out_ref[...] = jnp.zeros_like(out_ref)
    for stream in range(3):
        tail = proj_ref[stream].astype(jnp.float32)
        out_ref[pl.ds(2 * stream, 2), :] = tail[14:16, :]


def edges(proj):
    channels = proj.shape[-1]
    return pl.pallas_call(
        edge_kernel,
        grid=(1,),
        in_specs=[pl.BlockSpec((3, 16, channels), lambda i: (0, ROWS // 16 - 1, 0))],
        out_specs=pl.BlockSpec((8, channels), lambda i: (0, 0)),
        out_shape=jax.ShapeDtypeStruct((8, channels), jnp.float32),
        compiler_params=params(16),
    )(held(proj))


STEP = 32


def lanes_of(width):
    return [pl.ds(at, ROWS) for at in range(0, width, ROWS)]


def inputs_at(ext_ref, stream, row, lanes):
    rows = ext_ref[stream, pl.ds(row, STEP + 8), lanes]
    return [rows[8:]] + [pltpu.roll(rows, tap, 0)[8:] for tap in (1, 2)]


def filtered(taps_ref, stream, lanes, shifted):
    rows = taps_ref[stream, :, lanes]
    return sum(rows[tap : tap + 1] * shifted[tap] for tap in range(3))


def gate_kernel(proj_ref, taps_ref, grad_ref, out_ref, ext_ref):
    for stream in range(3):
        ext_ref[stream, pl.ds(8, ROWS), :] = proj_ref[stream].astype(jnp.float32)
        ext_ref[stream, pl.ds(0, 8), :] = jnp.zeros((8, grad_ref.shape[1]), jnp.float32)
    width = out_ref.shape[2]
    per = ROWS // width
    for at, lanes in enumerate(lanes_of(grad_ref.shape[1])):
        gated, grad_gate = [], []
        for row in range(0, ROWS, STEP):
            query, key, value = (
                filtered(taps_ref, stream, lanes, inputs_at(ext_ref, stream, row, lanes))
                for stream in range(3)
            )
            grad = grad_ref[pl.ds(row, STEP), lanes].astype(jnp.float32)
            gated.append((key * value).astype(jnp.bfloat16))
            grad_gate.append((grad * query).astype(jnp.bfloat16))
        for which, parts in enumerate((gated, grad_gate)):
            turned = jnp.concatenate(parts, axis=0).T
            out_ref[pl.ds(at * per, per), which] = turned.reshape(per, width, ROWS)


def gates(proj, taps, grad_out, width):
    channels = proj.shape[-1]
    block = min(2048, channels)
    return pl.pallas_call(
        gate_kernel,
        grid=(channels // block,),
        in_specs=[
            pl.BlockSpec((3, ROWS, block), lambda i: (0, 0, i)),
            pl.BlockSpec((3, 3, block), lambda i: (0, 0, i)),
            pl.BlockSpec((ROWS, block), lambda i: (0, i)),
        ],
        out_specs=pl.BlockSpec((block // width, 2, width, ROWS), lambda i: (i, 0, 0, 0)),
        out_shape=jax.ShapeDtypeStruct((channels // width, 2, width, ROWS), jnp.bfloat16),
        scratch_shapes=[pltpu.VMEM((3, ROWS + 8, block), jnp.float32)],
        compiler_params=params(32),
        cost_estimate=pl.CostEstimate(
            flops=40 * ROWS * channels, bytes_accessed=12 * ROWS * channels, transcendentals=0
        ),
    )(held(proj), taps, held(grad_out))


def head_kernel(rough_ref, proj_ref, edge_ref, taps_ref, grad_ref, out_ref):
    per, _, width, _ = out_ref.shape
    block = per * width
    features = []
    for stream in range(3):
        before = edge_ref[pl.ds(2 * stream, 2), :]
        rows = jnp.concatenate([before, proj_ref[stream].astype(jnp.float32)[:2]], axis=0)
        features.append(
            sum(taps_ref[stream, pl.ds(tap, 1), :] * rows[2 - tap : 4 - tap] for tap in range(3))
        )
    query, key, value = features
    grad = grad_ref[...].astype(jnp.float32)[:2]
    below = jnp.zeros((ROWS - 2, block), jnp.float32)
    head = lax.broadcasted_iota(jnp.int32, (block, ROWS), 1) < 2
    for which, rows in enumerate((key * value, grad * query)):
        turned = jnp.concatenate([rows, below], axis=0).astype(jnp.bfloat16).T
        kept = rough_ref[:, which].reshape(block, ROWS)
        out_ref[:, which] = jnp.where(head, turned, kept).reshape(per, width, ROWS)


def headed(rough, proj, edge, taps, grad_out):
    channels = proj.shape[-1]
    width = rough.shape[2]
    block = min(2048, channels)
    shape = (block // width, 2, width, ROWS)
    return pl.pallas_call(
        head_kernel,
        grid=(channels // block,),
        in_specs=[
            pl.BlockSpec(shape, lambda i: (i, 0, 0, 0)),
            pl.BlockSpec((3, 16, block), lambda i: (0, 0, i)),
            pl.BlockSpec((8, block), lambda i: (0, i)),
            pl.BlockSpec((3, 3, block), lambda i: (0, 0, i)),
            pl.BlockSpec((16, block), lambda i: (0, i)),
        ],
        out_specs=pl.BlockSpec(shape, lambda i: (i, 0, 0, 0)),
        out_shape=pltpu.HBM(rough.shape, jnp.bfloat16),
        compiler_params=params(32),
    )(rough, held(proj), edge, taps, held(grad_out))


def spectrum_kernel(filter_ref, fwd_a_ref, turn_ref, fwd_b_ref, out_ref):
    cos_w, sin_w = turn_ref[0], turn_ref[1]

    def one(ch, carry):
        high, low = split(filter_ref[ch])
        y = dot(fwd_a_ref[...], jnp.concatenate([high, high], axis=0))
        y += dot(fwd_a_ref[...], jnp.concatenate([low, low], axis=0))
        y_re, y_im = y[:ROWS], y[ROWS:]
        turned = jnp.concatenate(
            [y_re * cos_w - y_im * sin_w, y_re * sin_w + y_im * cos_w], axis=1
        )
        high, low = split(turned)
        out_ref[ch] = dot(high, fwd_b_ref[0]) + dot(high, fwd_b_ref[1]) + dot(low, fwd_b_ref[0])
        return carry

    lax.fori_loop(0, filter_ref.shape[0], one, 0, unroll=2)


def whole(shape):
    return pl.BlockSpec(shape, lambda *_: (0,) * len(shape))


def spectrum(filter_sq, tab):
    width = filter_sq.shape[0]
    block = min(8, width)
    return pl.pallas_call(
        spectrum_kernel,
        grid=(width // block,),
        in_specs=[
            pl.BlockSpec((block, ROWS, ROWS), lambda i: (i, 0, 0)),
            whole((2 * ROWS, 2 * ROWS)),
            whole((2, ROWS, ROWS)),
            whole((2, 2 * ROWS, 2 * ROWS)),
        ],
        out_specs=pl.BlockSpec((block, ROWS, 2 * ROWS), lambda i: (i, 0, 0)),
        out_shape=pltpu.HBM((width, ROWS, 2 * ROWS), jnp.float32),
        compiler_params=params(32),
        cost_estimate=pl.CostEstimate(
            flops=width * 5 * 2 * (2 * ROWS) ** 3, bytes_accessed=width * 3 * 4 * ROWS**2,
            transcendentals=0,
        ),
    )(filter_sq, tab["fwd_a"], tab["turn"], tab["fwd_b"])


def apply_right(rows, table_ref):
    total = dot(rows, table_ref[0])
    for term in range(1, table_ref.shape[0]):
        total += dot(rows, table_ref[term])
    return total


def apply_left(table_ref, columns):
    total = dot(table_ref[0], columns)
    for term in range(1, table_ref.shape[0]):
        total += dot(table_ref[term], columns)
    return total


def side(left, right):
    return jnp.concatenate([left.astype(jnp.bfloat16), right.astype(jnp.bfloat16)], axis=1)


def turned_back(spectra, inv_b_ref, inv_a_ref, cos_w, sin_w):
    v = apply_right(spectra, inv_b_ref)
    parts_re, parts_im = [], []
    for at in range(spectra.shape[0] // ROWS):
        v_re, v_im = halves(v[at * ROWS : (at + 1) * ROWS])
        parts_re.append((v_re * cos_w + v_im * sin_w).astype(jnp.bfloat16))
        parts_im.append((v_im * cos_w - v_re * sin_w).astype(jnp.bfloat16))
    parts = [jnp.concatenate(parts_re, axis=1), jnp.concatenate(parts_im, axis=1)]
    return apply_left(inv_a_ref, jnp.concatenate(parts, axis=0))


def conv_kernel(
    in_ref, spec_ref, fwd_a_ref, turn_ref, fwd_b_ref, inv_b_ref, inv_a_ref,
    out_ref, lag_ref, rows_ref, outs_ref, *, group,
):
    block = out_ref.shape[2]
    pitch = rows_ref.shape[1] // ROWS
    part = pl.program_id(1)
    here = pl.ds(pl.multiple_of(pl.program_id(0) * block, block), block)

    @pl.when(part == 0)
    def _():
        for at in range(2):
            rows = in_ref[:, at, here].astype(jnp.float32)
            spare = jnp.zeros((ROWS, pitch - block, ROWS), jnp.float32)
            rows_ref[at] = jnp.concatenate([rows, spare], axis=1).reshape(ROWS * pitch, ROWS)

    cos_w, sin_w = turn_ref[0], turn_ref[1]

    def some():
        chans = [part * group + at for at in range(group)]
        places = [(at, pl.ds(ch, ROWS, stride=pitch)) for ch in chans for at in range(2)]
        rows = [rows_ref[at, strided, :].astype(jnp.bfloat16) for at, strided in places]
        columns = jnp.concatenate(rows, axis=1)
        y = dot(fwd_a_ref[...], jnp.concatenate([columns, columns], axis=0))
        turned = []
        for at in range(2 * group):
            y_re = y[:ROWS, at * ROWS : (at + 1) * ROWS]
            y_im = y[ROWS:, at * ROWS : (at + 1) * ROWS]
            turned.append(side(y_re * cos_w - y_im * sin_w, y_re * sin_w + y_im * cos_w))
        z = apply_right(jnp.concatenate(turned, axis=0), fwd_b_ref)
        products = []
        for at in range(group):
            x_re, x_im = halves(z[2 * at * ROWS : (2 * at + 1) * ROWS])
            g_re, g_im = halves(z[(2 * at + 1) * ROWS : (2 * at + 2) * ROWS])
            h_re, h_im = halves(spec_ref[at])
            lag_ref[at] = side(g_re * x_re + g_im * x_im, g_im * x_re - g_re * x_im)
            products.append(side(x_re * h_re - x_im * h_im, x_re * h_im + x_im * h_re))
            products.append(side(h_re * g_re + h_im * g_im, h_re * g_im - h_im * g_re))
        res = turned_back(jnp.concatenate(products, axis=0), inv_b_ref, inv_a_ref, cos_w, sin_w)
        for column, (at, strided) in enumerate(places):
            outs_ref[at, strided, :] = res[:, column * ROWS : (column + 1) * ROWS]

    some()

    @pl.when(part == pl.num_programs(1) - 1)
    def _():
        for at in range(2):
            rows = outs_ref[at].reshape(ROWS, pitch, ROWS)[:, :block]
            out_ref[:, at] = rows.astype(jnp.bfloat16)


def convolve(received, spec, tab, group=8, block=16):
    width = received.shape[2]
    names = ("fwd_a", "turn", "fwd_b_high", "inv_b_high", "inv_a_high")
    return pl.pallas_call(
        functools.partial(conv_kernel, group=group),
        grid=(width // block, block // group),
        in_specs=[
            pl.BlockSpec(memory_space=pltpu.VMEM),
            pl.BlockSpec((group, ROWS, 2 * ROWS), lambda i, j: (i * (block // group) + j, 0, 0)),
        ]
        + [whole(tab[name].shape) for name in names],
        out_specs=[
            pl.BlockSpec((ROWS, 2, block, ROWS), lambda i, j: (0, 0, i, 0)),
            pl.BlockSpec((group, ROWS, 2 * ROWS), lambda i, j: (i * (block // group) + j, 0, 0)),
        ],
        out_shape=[
            pltpu.HBM((ROWS, 2, width, ROWS), jnp.bfloat16),
            pltpu.HBM((width, ROWS, 2 * ROWS), jnp.bfloat16),
        ],
        scratch_shapes=[pltpu.VMEM((2, ROWS * (block + 8), ROWS), jnp.float32)] * 2,
        compiler_params=params(40),
    )(received, held(spec), *(tab[name] for name in names))


def lag_kernel(products_ref, turn_ref, inv_b_ref, inv_a_ref, out_ref):
    count = products_ref.shape[0]
    products = products_ref[...].reshape(count * ROWS, 2 * ROWS)
    res = turned_back(products, inv_b_ref, inv_a_ref, turn_ref[0], turn_ref[1])
    for ch in range(count):
        out_ref[ch] = res[:, ch * ROWS : (ch + 1) * ROWS]


def lags(products, tab):
    width = products.shape[0]
    block = min(8, width)
    names = ("turn", "inv_b", "inv_a")
    return pl.pallas_call(
        lag_kernel,
        grid=(width // block,),
        in_specs=[pl.BlockSpec((block, ROWS, 2 * ROWS), lambda i: (i, 0, 0))]
        + [whole(tab[name].shape) for name in names],
        out_specs=pl.BlockSpec((block, ROWS, ROWS), lambda i: (i, 0, 0)),
        out_shape=jax.ShapeDtypeStruct((width, ROWS, ROWS), jnp.float32),
        compiler_params=params(32),
        cost_estimate=pl.CostEstimate(
            flops=width * 4 * 2 * (2 * ROWS) ** 3, bytes_accessed=width * 8 * ROWS**2,
            transcendentals=0,
        ),
    )(products, *(tab[name] for name in names))


def fill_turned(turned_ref, ret_ref):
    block = turned_ref.shape[2]
    for at in range(2):
        turned_ref[at] = ret_ref[:, at].reshape(block, ROWS).T.astype(jnp.float32)


def grads_at(turned_ref, taps_ref, grad_ref, row, lanes, keys, values):
    rows = pl.ds(row, STEP)
    conv, corr = turned_ref[0, rows, lanes], turned_ref[1, rows, lanes]
    key = filtered(taps_ref, 1, lanes, keys)
    value = filtered(taps_ref, 2, lanes, values)
    return (grad_ref[rows, lanes].astype(jnp.float32) * conv, corr * value, corr * key)


def sums_kernel(
    ret_ref, proj_ref, edge_ref, taps_ref, grad_ref, sums_ref, first_ref, ext_ref, turned_ref
):
    block = grad_ref.shape[1]
    channels = pl.ds(pl.multiple_of(pl.program_id(0) * block, block), block)
    fill_ext(ext_ref, proj_ref.at[:, :, channels], edge_ref)
    fill_turned(turned_ref, ret_ref)
    first_ref[...] = jnp.zeros_like(first_ref)
    sums_ref[...] = jnp.zeros_like(sums_ref)
    for at, lanes in enumerate(lanes_of(grad_ref.shape[1])):
        sums = [jnp.zeros((8, ROWS), jnp.float32)] * 9
        for row in range(0, ROWS, STEP):
            shifted = [inputs_at(ext_ref, stream, row, lanes) for stream in range(3)]
            grads = grads_at(turned_ref, taps_ref, grad_ref, row, lanes, shifted[1], shifted[2])
            for stream in range(3):
                for tap in range(3):
                    terms = (grads[stream] * shifted[stream][tap]).reshape(STEP // 8, 8, ROWS)
                    sums[3 * stream + tap] = sums[3 * stream + tap] + jnp.sum(terms, axis=0)
                if row == 0:
                    first_ref[pl.ds(2 * stream, 2), lanes] = grads[stream][:2]
        for which in range(9):
            sums_ref[which, pl.ds(at, 1)] = jnp.sum(sums[which], axis=0, keepdims=True)


def local_specs(block, width):
    return [
        pl.BlockSpec((block // width, 2, width, ROWS), lambda i: (i, 0, 0, 0)),
        pl.BlockSpec((3, ROWS, block), lambda i: (0, 0, i)),
        pl.BlockSpec((8, block), lambda i: (0, i)),
        pl.BlockSpec((3, 3, block), lambda i: (0, 0, i)),
        pl.BlockSpec((ROWS, block), lambda i: (0, i)),
    ]


def tap_sums(returned, proj, edge, taps, grad_out):
    channels = proj.shape[-1]
    block = min(1024, channels)
    specs = local_specs(block, returned.shape[2])
    specs[1] = pl.BlockSpec(memory_space=pltpu.VMEM)
    return pl.pallas_call(
        sums_kernel,
        grid=(channels // block,),
        in_specs=specs,
        out_specs=[
            pl.BlockSpec((16, block // ROWS, ROWS), lambda i: (0, i, 0)),
            pl.BlockSpec((8, block), lambda i: (0, i)),
        ],
        out_shape=[
            pltpu.HBM((16, channels // ROWS, ROWS), jnp.float32),
            pltpu.HBM((8, channels), jnp.float32),
        ],
        scratch_shapes=[
            pltpu.VMEM((3, ROWS + 8, block), jnp.float32),
            pltpu.VMEM((2, ROWS, block), jnp.float32),
        ],
        compiler_params=params(40),
    )(returned, proj, edge, taps, held(grad_out))


def grads_kernel(
    ret_ref, proj_ref, edge_ref, taps_ref, grad_ref, later_ref,
    out_ref, ext_ref, turned_ref, grads_ref,
):
    fill_ext(ext_ref, proj_ref, edge_ref)
    fill_turned(turned_ref, ret_ref)
    for stream in range(3):
        grads_ref[stream, pl.ds(ROWS, 2), :] = later_ref[pl.ds(2 * stream, 2), :]
    for lanes in lanes_of(grad_ref.shape[1]):
        for row in range(0, ROWS, STEP):
            shifted = [inputs_at(ext_ref, stream, row, lanes) for stream in (1, 2)]
            grads = grads_at(turned_ref, taps_ref, grad_ref, row, lanes, *shifted)
            for stream in range(3):
                grads_ref[stream, pl.ds(row, STEP), lanes] = grads[stream]
        for stream in range(3):
            for row in range(0, ROWS, STEP):
                ahead = [grads_ref[stream, pl.ds(row + tap, STEP), lanes] for tap in range(3)]
                total = filtered(taps_ref, stream, lanes, ahead)
                out_ref[stream, pl.ds(row, STEP), lanes] = total.astype(jnp.bfloat16)


def stream_grads(returned, proj, edge, taps, grad_out, later):
    channels = proj.shape[-1]
    block = min(1024, channels)
    return pl.pallas_call(
        grads_kernel,
        grid=(channels // block,),
        in_specs=local_specs(block, returned.shape[2])
        + [pl.BlockSpec((8, block), lambda i: (0, i))],
        out_specs=pl.BlockSpec((3, ROWS, block), lambda i: (0, 0, i)),
        out_shape=jax.ShapeDtypeStruct((3, ROWS, channels), jnp.bfloat16),
        scratch_shapes=[
            pltpu.VMEM((3, ROWS + 8, block), jnp.float32),
            pltpu.VMEM((2, ROWS, block), jnp.float32),
            pltpu.VMEM((3, ROWS + 8, block), jnp.float32),
        ],
        compiler_params=params(40),
        cost_estimate=pl.CostEstimate(
            flops=60 * ROWS * channels, bytes_accessed=18 * ROWS * channels, transcendentals=0
        ),
    )(returned, held(proj), edge, taps, held(grad_out), later)


def passed_along(value, steps):
    count = lax.axis_size("ctx")
    initial, last = (max(0, -steps), min(count, count - steps))
    return lax.ppermute(value, "ctx", [(source, source + steps) for source in range(initial, last)])


def exchanged(value, axes):
    return lax.all_to_all(value, axes, split_axis=0, concat_axis=0, tiled=True)


def sum_everywhere(sums, beside):
    channels = sums.shape[1] * ROWS
    devices = lax.axis_size("dp") * lax.axis_size("ctx")
    pieces = sums.reshape(devices, 2, ROWS)
    own = jnp.sum(exchanged(pieces, ("dp", "ctx")), axis=0)
    own, beside = lax.optimization_barrier((own.astype(jnp.bfloat16), beside))
    spread = exchanged(jnp.broadcast_to(own[None], pieces.shape), ("dp", "ctx"))
    return spread.reshape(16, channels)[:9].reshape(3, 3, channels).astype(jnp.float32), beside


def local(projected, short_taps, long_filter, grad_out):
    tab = tables()
    proj = projected[:, 0]
    grad_rows = grad_out[0]
    width = long_filter.shape[0]
    edge = passed_along(edges(proj), 1)
    rough = gates(proj, short_taps, grad_rows, width)
    sent = headed(rough, proj, edge, short_taps, grad_rows)
    received = exchanged(sent, "ctx")
    spec = spectrum(long_filter.reshape(width, ROWS, ROWS), tab)
    results, products = convolve(received, spec, tab)
    returned = exchanged(results, "ctx")
    lag = lags(products, tab)
    second = lax.axis_index("dp") == 1
    lower, upper = lag[:, : ROWS // 2], lag[:, ROWS // 2 :]
    other = lax.ppermute(
        jnp.where(second, lower, upper).astype(jnp.bfloat16), "dp", [(0, 1), (1, 0)]
    )
    lag_sum = jnp.where(second, upper, lower) + other.astype(jnp.float32)
    grad_filter = lag_sum.reshape(width, ROWS // 2 * ROWS)
    late_edge, grad_filter = lax.optimization_barrier((edge, grad_filter))
    sums, first = tap_sums(returned, proj, late_edge, short_taps, grad_rows)
    grad_taps, later = sum_everywhere(sums, passed_along(first, -1))
    grad_in = stream_grads(returned, proj, edge, short_taps, grad_rows, later)
    return (grad_in[:, None], grad_taps, grad_filter)


def solution(mesh):
    return jax.shard_map(
        local,
        mesh=mesh,
        in_specs=(P(None, "dp", "ctx", None), P(), P("ctx", None), P("dp", "ctx", None)),
        out_specs=(P(None, "dp", "ctx", None), P(), P("ctx", "dp")),
        check_vma=False,
    )
```

```python
import functools
import math

import jax
import jax.numpy as jnp
import numpy as np
from jax import lax
from jax.experimental import pallas as pl
from jax.experimental.pallas import tpu as pltpu
from jax.sharding import PartitionSpec as P

ROWS = 128
MIB = 2**20


def rounded(table):
    high = table.astype(jnp.bfloat16)
    low = (table - high.astype(np.float64)).astype(jnp.bfloat16)
    return high, low


@functools.cache
def tables():
    idx = np.arange(ROWS, dtype=np.float64)
    quarter = idx + 0.25
    ang_a = 2.0 * math.pi * np.outer(quarter, idx) / ROWS
    fwd_a = np.concatenate([np.cos(ang_a), -np.sin(ang_a)], axis=0)
    inv_a = np.concatenate([np.cos(ang_a.T), -np.sin(ang_a.T)], axis=1) / ROWS**2
    ang_w = 2.0 * math.pi * np.outer(quarter, idx) / ROWS**2
    turn = np.stack([np.cos(ang_w), -np.sin(ang_w)]).astype(np.float32)
    ang_b = 2.0 * math.pi * (np.outer(idx, idx) % ROWS) / ROWS
    cos_b, sin_b = np.cos(ang_b), np.sin(ang_b)
    fwd_b = np.block([[cos_b, -sin_b], [sin_b, cos_b]])
    inv_b = np.block([[cos_b, sin_b], [-sin_b, cos_b]])
    return {
        "fwd_a": np.concatenate(rounded(fwd_a), axis=1),
        "turn": turn,
        "fwd_b": np.stack(rounded(fwd_b)),
        "fwd_b_high": np.stack(rounded(fwd_b)[:1]),
        "inv_b": np.stack(rounded(inv_b)),
        "inv_b_high": np.stack(rounded(inv_b)[:1]),
        "inv_a": np.stack(rounded(inv_a)),
        "inv_a_high": np.stack(rounded(inv_a)[:1]),
    }


def dot(lhs, rhs):
    return lax.dot_general(lhs, rhs, (((1,), (0,)), ((), ())), preferred_element_type=jnp.float32)


def split(value):
    high = value.astype(jnp.bfloat16)
    return high, (value - high.astype(jnp.float32)).astype(jnp.bfloat16)


def halves(value):
    return value[:, :ROWS], value[:, ROWS:]


def held(value):
    return pltpu.with_memory_space_constraint(value, pltpu.HBM)


def params(mib=48):
    return pltpu.CompilerParams(vmem_limit_bytes=mib * MIB)


def fill_ext(ext_ref, proj_ref, edge_ref):
    for stream in range(3):
        ext_ref[stream, pl.ds(8, ROWS), :] = proj_ref[stream].astype(jnp.float32)
        ext_ref[stream, pl.ds(6, 2), :] = edge_ref[pl.ds(2 * stream, 2), :]


def edge_kernel(proj_ref, out_ref):
    out_ref[...] = jnp.zeros_like(out_ref)
    for stream in range(3):
        tail = proj_ref[stream].astype(jnp.float32)
        out_ref[pl.ds(2 * stream, 2), :] = tail[14:16, :]


def edges(proj):
    channels = proj.shape[-1]
    return pl.pallas_call(
        edge_kernel,
        grid=(1,),
        in_specs=[pl.BlockSpec((3, 16, channels), lambda i: (0, ROWS // 16 - 1, 0))],
        out_specs=pl.BlockSpec((8, channels), lambda i: (0, 0)),
        out_shape=jax.ShapeDtypeStruct((8, channels), jnp.float32),
        compiler_params=params(16),
    )(held(proj))


STEP = 32


def lanes_of(width):
    return [pl.ds(at, ROWS) for at in range(0, width, ROWS)]


def inputs_at(ext_ref, stream, row, lanes):
    rows = ext_ref[stream, pl.ds(row, STEP + 8), lanes]
    return [rows[8:]] + [pltpu.roll(rows, tap, 0)[8:] for tap in (1, 2)]


def filtered(taps_ref, stream, lanes, shifted):
    rows = taps_ref[stream, :, lanes]
    return sum(rows[tap : tap + 1] * shifted[tap] for tap in range(3))


def gate_kernel(proj_ref, taps_ref, grad_ref, out_ref, ext_ref):
    for stream in range(3):
        ext_ref[stream, pl.ds(8, ROWS), :] = proj_ref[stream].astype(jnp.float32)
        ext_ref[stream, pl.ds(0, 8), :] = jnp.zeros((8, grad_ref.shape[1]), jnp.float32)
    width = out_ref.shape[2]
    per = ROWS // width
    for at, lanes in enumerate(lanes_of(grad_ref.shape[1])):
        gated, grad_gate = [], []
        for row in range(0, ROWS, STEP):
            query, key, value = (
                filtered(taps_ref, stream, lanes, inputs_at(ext_ref, stream, row, lanes))
                for stream in range(3)
            )
            grad = grad_ref[pl.ds(row, STEP), lanes].astype(jnp.float32)
            gated.append((key * value).astype(jnp.bfloat16))
            grad_gate.append((grad * query).astype(jnp.bfloat16))
        for which, parts in enumerate((gated, grad_gate)):
            turned = jnp.concatenate(parts, axis=0).T
            out_ref[pl.ds(at * per, per), which] = turned.reshape(per, width, ROWS)


def gates(proj, taps, grad_out, width):
    channels = proj.shape[-1]
    block = min(2048, channels)
    return pl.pallas_call(
        gate_kernel,
        grid=(channels // block,),
        in_specs=[
            pl.BlockSpec((3, ROWS, block), lambda i: (0, 0, i)),
            pl.BlockSpec((3, 3, block), lambda i: (0, 0, i)),
            pl.BlockSpec((ROWS, block), lambda i: (0, i)),
        ],
        out_specs=pl.BlockSpec((block // width, 2, width, ROWS), lambda i: (i, 0, 0, 0)),
        out_shape=jax.ShapeDtypeStruct((channels // width, 2, width, ROWS), jnp.bfloat16),
        scratch_shapes=[pltpu.VMEM((3, ROWS + 8, block), jnp.float32)],
        compiler_params=params(32),
        cost_estimate=pl.CostEstimate(
            flops=40 * ROWS * channels, bytes_accessed=12 * ROWS * channels, transcendentals=0
        ),
    )(held(proj), taps, held(grad_out))


def head_kernel(rough_ref, proj_ref, edge_ref, taps_ref, grad_ref, out_ref):
    per, _, width, _ = out_ref.shape
    block = per * width
    features = []
    for stream in range(3):
        before = edge_ref[pl.ds(2 * stream, 2), :]
        rows = jnp.concatenate([before, proj_ref[stream].astype(jnp.float32)[:2]], axis=0)
        features.append(
            sum(taps_ref[stream, pl.ds(tap, 1), :] * rows[2 - tap : 4 - tap] for tap in range(3))
        )
    query, key, value = features
    grad = grad_ref[...].astype(jnp.float32)[:2]
    below = jnp.zeros((ROWS - 2, block), jnp.float32)
    head = lax.broadcasted_iota(jnp.int32, (block, ROWS), 1) < 2
    for which, rows in enumerate((key * value, grad * query)):
        turned = jnp.concatenate([rows, below], axis=0).astype(jnp.bfloat16).T
        kept = rough_ref[:, which].reshape(block, ROWS)
        out_ref[:, which] = jnp.where(head, turned, kept).reshape(per, width, ROWS)


def headed(rough, proj, edge, taps, grad_out):
    channels = proj.shape[-1]
    width = rough.shape[2]
    block = min(2048, channels)
    shape = (block // width, 2, width, ROWS)
    return pl.pallas_call(
        head_kernel,
        grid=(channels // block,),
        in_specs=[
            pl.BlockSpec(shape, lambda i: (i, 0, 0, 0)),
            pl.BlockSpec((3, 16, block), lambda i: (0, 0, i)),
            pl.BlockSpec((8, block), lambda i: (0, i)),
            pl.BlockSpec((3, 3, block), lambda i: (0, 0, i)),
            pl.BlockSpec((16, block), lambda i: (0, i)),
        ],
        out_specs=pl.BlockSpec(shape, lambda i: (i, 0, 0, 0)),
        out_shape=pltpu.HBM(rough.shape, jnp.bfloat16),
        compiler_params=params(32),
    )(rough, held(proj), edge, taps, held(grad_out))


def spectrum_kernel(filter_ref, fwd_a_ref, turn_ref, fwd_b_ref, out_ref):
    cos_w, sin_w = turn_ref[0], turn_ref[1]

    def one(ch, carry):
        high, low = split(filter_ref[ch])
        y = dot(fwd_a_ref[...], jnp.concatenate([high, high], axis=0))
        y += dot(fwd_a_ref[...], jnp.concatenate([low, low], axis=0))
        y_re, y_im = y[:ROWS], y[ROWS:]
        turned = jnp.concatenate(
            [y_re * cos_w - y_im * sin_w, y_re * sin_w + y_im * cos_w], axis=1
        )
        high, low = split(turned)
        out_ref[ch] = dot(high, fwd_b_ref[0]) + dot(high, fwd_b_ref[1]) + dot(low, fwd_b_ref[0])
        return carry

    lax.fori_loop(0, filter_ref.shape[0], one, 0, unroll=2)


def whole(shape):
    return pl.BlockSpec(shape, lambda *_: (0,) * len(shape))


def spectrum(filter_sq, tab):
    width = filter_sq.shape[0]
    block = min(8, width)
    return pl.pallas_call(
        spectrum_kernel,
        grid=(width // block,),
        in_specs=[
            pl.BlockSpec((block, ROWS, ROWS), lambda i: (i, 0, 0)),
            whole((2 * ROWS, 2 * ROWS)),
            whole((2, ROWS, ROWS)),
            whole((2, 2 * ROWS, 2 * ROWS)),
        ],
        out_specs=pl.BlockSpec((block, ROWS, 2 * ROWS), lambda i: (i, 0, 0)),
        out_shape=pltpu.HBM((width, ROWS, 2 * ROWS), jnp.float32),
        compiler_params=params(32),
        cost_estimate=pl.CostEstimate(
            flops=width * 5 * 2 * (2 * ROWS) ** 3, bytes_accessed=width * 3 * 4 * ROWS**2,
            transcendentals=0,
        ),
    )(filter_sq, tab["fwd_a"], tab["turn"], tab["fwd_b"])


def apply_right(rows, table_ref):
    total = dot(rows, table_ref[0])
    for term in range(1, table_ref.shape[0]):
        total += dot(rows, table_ref[term])
    return total


def apply_left(table_ref, columns):
    total = dot(table_ref[0], columns)
    for term in range(1, table_ref.shape[0]):
        total += dot(table_ref[term], columns)
    return total


def side(left, right):
    return jnp.concatenate([left.astype(jnp.bfloat16), right.astype(jnp.bfloat16)], axis=1)


def turned_back(spectra, inv_b_ref, inv_a_ref, cos_w, sin_w):
    v = apply_right(spectra, inv_b_ref)
    parts_re, parts_im = [], []
    for at in range(spectra.shape[0] // ROWS):
        v_re, v_im = halves(v[at * ROWS : (at + 1) * ROWS])
        parts_re.append((v_re * cos_w + v_im * sin_w).astype(jnp.bfloat16))
        parts_im.append((v_im * cos_w - v_re * sin_w).astype(jnp.bfloat16))
    parts = [jnp.concatenate(parts_re, axis=1), jnp.concatenate(parts_im, axis=1)]
    return apply_left(inv_a_ref, jnp.concatenate(parts, axis=0))


def conv_kernel(
    in_ref, spec_ref, fwd_a_ref, turn_ref, fwd_b_ref, inv_b_ref, inv_a_ref,
    out_ref, lag_ref, rows_ref, outs_ref, *, group,
):
    block = out_ref.shape[2]
    pitch = rows_ref.shape[1] // ROWS
    part = pl.program_id(1)
    here = pl.ds(pl.multiple_of(pl.program_id(0) * block, block), block)

    @pl.when(part == 0)
    def _():
        for at in range(2):
            rows = in_ref[:, at, here].astype(jnp.float32)
            spare = jnp.zeros((ROWS, pitch - block, ROWS), jnp.float32)
            rows_ref[at] = jnp.concatenate([rows, spare], axis=1).reshape(ROWS * pitch, ROWS)

    cos_w, sin_w = turn_ref[0], turn_ref[1]

    def some():
        chans = [part * group + at for at in range(group)]
        places = [(at, pl.ds(ch, ROWS, stride=pitch)) for ch in chans for at in range(2)]
        rows = [rows_ref[at, strided, :].astype(jnp.bfloat16) for at, strided in places]
        columns = jnp.concatenate(rows, axis=1)
        y = dot(fwd_a_ref[...], jnp.concatenate([columns, columns], axis=0))
        turned = []
        for at in range(2 * group):
            y_re = y[:ROWS, at * ROWS : (at + 1) * ROWS]
            y_im = y[ROWS:, at * ROWS : (at + 1) * ROWS]
            turned.append(side(y_re * cos_w - y_im * sin_w, y_re * sin_w + y_im * cos_w))
        z = apply_right(jnp.concatenate(turned, axis=0), fwd_b_ref)
        products = []
        for at in range(group):
            x_re, x_im = halves(z[2 * at * ROWS : (2 * at + 1) * ROWS])
            g_re, g_im = halves(z[(2 * at + 1) * ROWS : (2 * at + 2) * ROWS])
            h_re, h_im = halves(spec_ref[at])
            lag_ref[at] = side(g_re * x_re + g_im * x_im, g_im * x_re - g_re * x_im)
            products.append(side(x_re * h_re - x_im * h_im, x_re * h_im + x_im * h_re))
            products.append(side(h_re * g_re + h_im * g_im, h_re * g_im - h_im * g_re))
        res = turned_back(jnp.concatenate(products, axis=0), inv_b_ref, inv_a_ref, cos_w, sin_w)
        for column, (at, strided) in enumerate(places):
            outs_ref[at, strided, :] = res[:, column * ROWS : (column + 1) * ROWS]

    some()

    @pl.when(part == pl.num_programs(1) - 1)
    def _():
        for at in range(2):
            rows = outs_ref[at].reshape(ROWS, pitch, ROWS)[:, :block]
            out_ref[:, at] = rows.astype(jnp.bfloat16)


def convolve(received, spec, tab, group=8, block=16):
    width = received.shape[2]
    names = ("fwd_a", "turn", "fwd_b_high", "inv_b_high", "inv_a_high")
    return pl.pallas_call(
        functools.partial(conv_kernel, group=group),
        grid=(width // block, block // group),
        in_specs=[
            pl.BlockSpec(memory_space=pltpu.VMEM),
            pl.BlockSpec((group, ROWS, 2 * ROWS), lambda i, j: (i * (block // group) + j, 0, 0)),
        ]
        + [whole(tab[name].shape) for name in names],
        out_specs=[
            pl.BlockSpec((ROWS, 2, block, ROWS), lambda i, j: (0, 0, i, 0)),
            pl.BlockSpec((group, ROWS, 2 * ROWS), lambda i, j: (i * (block // group) + j, 0, 0)),
        ],
        out_shape=[
            pltpu.HBM((ROWS, 2, width, ROWS), jnp.bfloat16),
            pltpu.HBM((width, ROWS, 2 * ROWS), jnp.bfloat16),
        ],
        scratch_shapes=[pltpu.VMEM((2, ROWS * (block + 8), ROWS), jnp.float32)] * 2,
        compiler_params=params(40),
    )(received, held(spec), *(tab[name] for name in names))


def lag_kernel(products_ref, turn_ref, inv_b_ref, inv_a_ref, out_ref):
    count = products_ref.shape[0]
    products = products_ref[...].reshape(count * ROWS, 2 * ROWS)
    res = turned_back(products, inv_b_ref, inv_a_ref, turn_ref[0], turn_ref[1])
    for ch in range(count):
        out_ref[ch] = res[:, ch * ROWS : (ch + 1) * ROWS]


def lags(products, tab):
    width = products.shape[0]
    block = min(8, width)
    names = ("turn", "inv_b", "inv_a")
    return pl.pallas_call(
        lag_kernel,
        grid=(width // block,),
        in_specs=[pl.BlockSpec((block, ROWS, 2 * ROWS), lambda i: (i, 0, 0))]
        + [whole(tab[name].shape) for name in names],
        out_specs=pl.BlockSpec((block, ROWS, ROWS), lambda i: (i, 0, 0)),
        out_shape=jax.ShapeDtypeStruct((width, ROWS, ROWS), jnp.float32),
        compiler_params=params(32),
        cost_estimate=pl.CostEstimate(
            flops=width * 4 * 2 * (2 * ROWS) ** 3, bytes_accessed=width * 8 * ROWS**2,
            transcendentals=0,
        ),
    )(products, *(tab[name] for name in names))


def fill_turned(turned_ref, ret_ref):
    block = turned_ref.shape[2]
    for at in range(2):
        turned_ref[at] = ret_ref[:, at].reshape(block, ROWS).T.astype(jnp.float32)


def grads_at(turned_ref, taps_ref, grad_ref, row, lanes, keys, values):
    rows = pl.ds(row, STEP)
    conv, corr = turned_ref[0, rows, lanes], turned_ref[1, rows, lanes]
    key = filtered(taps_ref, 1, lanes, keys)
    value = filtered(taps_ref, 2, lanes, values)
    return (grad_ref[rows, lanes].astype(jnp.float32) * conv, corr * value, corr * key)


def sums_kernel(
    ret_ref, proj_ref, edge_ref, taps_ref, grad_ref, sums_ref, first_ref, ext_ref, turned_ref
):
    block = grad_ref.shape[1]
    channels = pl.ds(pl.multiple_of(pl.program_id(0) * block, block), block)
    fill_ext(ext_ref, proj_ref.at[:, :, channels], edge_ref)
    fill_turned(turned_ref, ret_ref)
    first_ref[...] = jnp.zeros_like(first_ref)
    sums_ref[...] = jnp.zeros_like(sums_ref)
    for at, lanes in enumerate(lanes_of(grad_ref.shape[1])):
        sums = [jnp.zeros((8, ROWS), jnp.float32)] * 9
        for row in range(0, ROWS, STEP):
            shifted = [inputs_at(ext_ref, stream, row, lanes) for stream in range(3)]
            grads = grads_at(turned_ref, taps_ref, grad_ref, row, lanes, shifted[1], shifted[2])
            for stream in range(3):
                for tap in range(3):
                    terms = (grads[stream] * shifted[stream][tap]).reshape(STEP // 8, 8, ROWS)
                    sums[3 * stream + tap] = sums[3 * stream + tap] + jnp.sum(terms, axis=0)
                if row == 0:
                    first_ref[pl.ds(2 * stream, 2), lanes] = grads[stream][:2]
        for which in range(9):
            sums_ref[which, pl.ds(at, 1)] = jnp.sum(sums[which], axis=0, keepdims=True)


def local_specs(block, width):
    return [
        pl.BlockSpec((block // width, 2, width, ROWS), lambda i: (i, 0, 0, 0)),
        pl.BlockSpec((3, ROWS, block), lambda i: (0, 0, i)),
        pl.BlockSpec((8, block), lambda i: (0, i)),
        pl.BlockSpec((3, 3, block), lambda i: (0, 0, i)),
        pl.BlockSpec((ROWS, block), lambda i: (0, i)),
    ]


def tap_sums(returned, proj, edge, taps, grad_out):
    channels = proj.shape[-1]
    block = min(2048, channels)
    specs = local_specs(block, returned.shape[2])
    specs[1] = pl.BlockSpec(memory_space=pltpu.VMEM)
    return pl.pallas_call(
        sums_kernel,
        grid=(channels // block,),
        in_specs=specs,
        out_specs=[
            pl.BlockSpec((16, block // ROWS, ROWS), lambda i: (0, i, 0)),
            pl.BlockSpec((8, block), lambda i: (0, i)),
        ],
        out_shape=[
            pltpu.HBM((16, channels // ROWS, ROWS), jnp.float32),
            pltpu.HBM((8, channels), jnp.float32),
        ],
        scratch_shapes=[
            pltpu.VMEM((3, ROWS + 8, block), jnp.float32),
            pltpu.VMEM((2, ROWS, block), jnp.float32),
        ],
        compiler_params=params(40),
    )(returned, proj, edge, taps, held(grad_out))


def grads_kernel(
    ret_ref, proj_ref, edge_ref, taps_ref, grad_ref, later_ref,
    out_ref, ext_ref, turned_ref, grads_ref,
):
    fill_ext(ext_ref, proj_ref, edge_ref)
    fill_turned(turned_ref, ret_ref)
    for stream in range(3):
        grads_ref[stream, pl.ds(ROWS, 2), :] = later_ref[pl.ds(2 * stream, 2), :]
    for lanes in lanes_of(grad_ref.shape[1]):
        for row in range(0, ROWS, STEP):
            shifted = [inputs_at(ext_ref, stream, row, lanes) for stream in (1, 2)]
            grads = grads_at(turned_ref, taps_ref, grad_ref, row, lanes, *shifted)
            for stream in range(3):
                grads_ref[stream, pl.ds(row, STEP), lanes] = grads[stream]
        for stream in range(3):
            for row in range(0, ROWS, STEP):
                ahead = [grads_ref[stream, pl.ds(row + tap, STEP), lanes] for tap in range(3)]
                total = filtered(taps_ref, stream, lanes, ahead)
                out_ref[stream, pl.ds(row, STEP), lanes] = total.astype(jnp.bfloat16)


def stream_grads(returned, proj, edge, taps, grad_out, later):
    channels = proj.shape[-1]
    block = min(1024, channels)
    return pl.pallas_call(
        grads_kernel,
        grid=(channels // block,),
        in_specs=local_specs(block, returned.shape[2])
        + [pl.BlockSpec((8, block), lambda i: (0, i))],
        out_specs=pl.BlockSpec((3, ROWS, block), lambda i: (0, 0, i)),
        out_shape=jax.ShapeDtypeStruct((3, ROWS, channels), jnp.bfloat16),
        scratch_shapes=[
            pltpu.VMEM((3, ROWS + 8, block), jnp.float32),
            pltpu.VMEM((2, ROWS, block), jnp.float32),
            pltpu.VMEM((3, ROWS + 8, block), jnp.float32),
        ],
        compiler_params=params(40),
        cost_estimate=pl.CostEstimate(
            flops=60 * ROWS * channels, bytes_accessed=18 * ROWS * channels, transcendentals=0
        ),
    )(returned, held(proj), edge, taps, held(grad_out), later)


def passed_along(value, steps):
    count = lax.axis_size("ctx")
    initial, last = (max(0, -steps), min(count, count - steps))
    return lax.ppermute(value, "ctx", [(source, source + steps) for source in range(initial, last)])


def exchanged(value, axes):
    return lax.all_to_all(value, axes, split_axis=0, concat_axis=0, tiled=True)


def sum_everywhere(sums, beside):
    channels = sums.shape[1] * ROWS
    devices = lax.axis_size("dp") * lax.axis_size("ctx")
    pieces = sums.reshape(devices, 2, ROWS)
    own = jnp.sum(exchanged(pieces, ("dp", "ctx")), axis=0)
    own, beside = lax.optimization_barrier((own.astype(jnp.bfloat16), beside))
    spread = exchanged(jnp.broadcast_to(own[None], pieces.shape), ("dp", "ctx"))
    return spread.reshape(16, channels)[:9].reshape(3, 3, channels).astype(jnp.float32), beside


def local(projected, short_taps, long_filter, grad_out):
    tab = tables()
    proj = projected[:, 0]
    grad_rows = grad_out[0]
    width = long_filter.shape[0]
    edge = passed_along(edges(proj), 1)
    rough = gates(proj, short_taps, grad_rows, width)
    sent = headed(rough, proj, edge, short_taps, grad_rows)
    received = exchanged(sent, "ctx")
    spec = spectrum(long_filter.reshape(width, ROWS, ROWS), tab)
    results, products = convolve(received, spec, tab)
    returned = exchanged(results, "ctx")
    lag = lags(products, tab)
    second = lax.axis_index("dp") == 1
    lower, upper = lag[:, : ROWS // 2], lag[:, ROWS // 2 :]
    other = lax.ppermute(
        jnp.where(second, lower, upper).astype(jnp.bfloat16), "dp", [(0, 1), (1, 0)]
    )
    lag_sum = jnp.where(second, upper, lower) + other.astype(jnp.float32)
    grad_filter = lag_sum.reshape(width, ROWS // 2 * ROWS)
    late_edge, grad_filter = lax.optimization_barrier((edge, grad_filter))
    sums, first = tap_sums(returned, proj, late_edge, short_taps, grad_rows)
    grad_taps, later = sum_everywhere(sums, passed_along(first, -1))
    grad_in = stream_grads(returned, proj, edge, short_taps, grad_rows, later)
    return (grad_in[:, None], grad_taps, grad_filter)


def solution(mesh):
    return jax.shard_map(
        local,
        mesh=mesh,
        in_specs=(P(None, "dp", "ctx", None), P(), P("ctx", None), P("dp", "ctx", None)),
        out_specs=(P(None, "dp", "ctx", None), P(), P("ctx", "dp")),
        check_vma=False,
    )
```

```python
import functools
import math

import jax
import jax.numpy as jnp
import numpy as np
from jax import lax
from jax.experimental import pallas as pl
from jax.experimental.pallas import tpu as pltpu
from jax.sharding import PartitionSpec as P

ROWS = 128
MIB = 2**20


def rounded(table):
    high = table.astype(jnp.bfloat16)
    low = (table - high.astype(np.float64)).astype(jnp.bfloat16)
    return high, low


@functools.cache
def tables():
    idx = np.arange(ROWS, dtype=np.float64)
    quarter = idx + 0.25
    ang_a = 2.0 * math.pi * np.outer(quarter, idx) / ROWS
    fwd_a = np.concatenate([np.cos(ang_a), -np.sin(ang_a)], axis=0)
    inv_a = np.concatenate([np.cos(ang_a.T), -np.sin(ang_a.T)], axis=1) / ROWS**2
    ang_w = 2.0 * math.pi * np.outer(quarter, idx) / ROWS**2
    turn = np.stack([np.cos(ang_w), -np.sin(ang_w)]).astype(np.float32)
    ang_b = 2.0 * math.pi * (np.outer(idx, idx) % ROWS) / ROWS
    cos_b, sin_b = np.cos(ang_b), np.sin(ang_b)
    fwd_b = np.block([[cos_b, -sin_b], [sin_b, cos_b]])
    inv_b = np.block([[cos_b, sin_b], [-sin_b, cos_b]])
    return {
        "fwd_a": np.concatenate(rounded(fwd_a), axis=1),
        "turn": turn,
        "fwd_b": np.stack(rounded(fwd_b)),
        "fwd_b_high": np.stack(rounded(fwd_b)[:1]),
        "inv_b": np.stack(rounded(inv_b)),
        "inv_b_high": np.stack(rounded(inv_b)[:1]),
        "inv_a": np.stack(rounded(inv_a)),
        "inv_a_high": np.stack(rounded(inv_a)[:1]),
    }


def dot(lhs, rhs):
    return lax.dot_general(lhs, rhs, (((1,), (0,)), ((), ())), preferred_element_type=jnp.float32)


def split(value):
    high = value.astype(jnp.bfloat16)
    return high, (value - high.astype(jnp.float32)).astype(jnp.bfloat16)


def halves(value):
    return value[:, :ROWS], value[:, ROWS:]


def held(value):
    return pltpu.with_memory_space_constraint(value, pltpu.HBM)


def params(mib=48):
    return pltpu.CompilerParams(vmem_limit_bytes=mib * MIB)


def fill_ext(ext_ref, proj_ref, edge_ref):
    for stream in range(3):
        ext_ref[stream, pl.ds(8, ROWS), :] = proj_ref[stream].astype(jnp.float32)
        ext_ref[stream, pl.ds(6, 2), :] = edge_ref[pl.ds(2 * stream, 2), :]


def edge_kernel(proj_ref, out_ref):
    out_ref[...] = jnp.zeros_like(out_ref)
    for stream in range(3):
        tail = proj_ref[stream].astype(jnp.float32)
        out_ref[pl.ds(2 * stream, 2), :] = tail[14:16, :]


def edges(proj):
    channels = proj.shape[-1]
    return pl.pallas_call(
        edge_kernel,
        grid=(1,),
        in_specs=[pl.BlockSpec((3, 16, channels), lambda i: (0, ROWS // 16 - 1, 0))],
        out_specs=pl.BlockSpec((8, channels), lambda i: (0, 0)),
        out_shape=jax.ShapeDtypeStruct((8, channels), jnp.float32),
        compiler_params=params(16),
    )(held(proj))


STEP = 32


def lanes_of(width):
    return [pl.ds(at, ROWS) for at in range(0, width, ROWS)]


def inputs_at(ext_ref, stream, row, lanes):
    rows = ext_ref[stream, pl.ds(row, STEP + 8), lanes]
    return [rows[8:]] + [pltpu.roll(rows, tap, 0)[8:] for tap in (1, 2)]


def filtered(taps_ref, stream, lanes, shifted):
    rows = taps_ref[stream, :, lanes]
    return sum(rows[tap : tap + 1] * shifted[tap] for tap in range(3))


def gate_kernel(proj_ref, taps_ref, grad_ref, out_ref, ext_ref):
    for stream in range(3):
        ext_ref[stream, pl.ds(8, ROWS), :] = proj_ref[stream].astype(jnp.float32)
        ext_ref[stream, pl.ds(0, 8), :] = jnp.zeros((8, grad_ref.shape[1]), jnp.float32)
    width = out_ref.shape[2]
    per = ROWS // width
    for at, lanes in enumerate(lanes_of(grad_ref.shape[1])):
        gated, grad_gate = [], []
        for row in range(0, ROWS, STEP):
            query, key, value = (
                filtered(taps_ref, stream, lanes, inputs_at(ext_ref, stream, row, lanes))
                for stream in range(3)
            )
            grad = grad_ref[pl.ds(row, STEP), lanes].astype(jnp.float32)
            gated.append((key * value).astype(jnp.bfloat16))
            grad_gate.append((grad * query).astype(jnp.bfloat16))
        for which, parts in enumerate((gated, grad_gate)):
            turned = jnp.concatenate(parts, axis=0).T
            out_ref[pl.ds(at * per, per), which] = turned.reshape(per, width, ROWS)


def gates(proj, taps, grad_out, width):
    channels = proj.shape[-1]
    block = min(2048, channels)
    return pl.pallas_call(
        gate_kernel,
        grid=(channels // block,),
        in_specs=[
            pl.BlockSpec((3, ROWS, block), lambda i: (0, 0, i)),
            pl.BlockSpec((3, 3, block), lambda i: (0, 0, i)),
            pl.BlockSpec((ROWS, block), lambda i: (0, i)),
        ],
        out_specs=pl.BlockSpec((block // width, 2, width, ROWS), lambda i: (i, 0, 0, 0)),
        out_shape=jax.ShapeDtypeStruct((channels // width, 2, width, ROWS), jnp.bfloat16),
        scratch_shapes=[pltpu.VMEM((3, ROWS + 8, block), jnp.float32)],
        compiler_params=params(32),
        cost_estimate=pl.CostEstimate(
            flops=40 * ROWS * channels, bytes_accessed=12 * ROWS * channels, transcendentals=0
        ),
    )(held(proj), taps, held(grad_out))


def head_kernel(rough_ref, proj_ref, edge_ref, taps_ref, grad_ref, out_ref):
    per, _, width, _ = out_ref.shape
    block = per * width
    features = []
    for stream in range(3):
        before = edge_ref[pl.ds(2 * stream, 2), :]
        rows = jnp.concatenate([before, proj_ref[stream].astype(jnp.float32)[:2]], axis=0)
        features.append(
            sum(taps_ref[stream, pl.ds(tap, 1), :] * rows[2 - tap : 4 - tap] for tap in range(3))
        )
    query, key, value = features
    grad = grad_ref[...].astype(jnp.float32)[:2]
    below = jnp.zeros((ROWS - 2, block), jnp.float32)
    head = lax.broadcasted_iota(jnp.int32, (block, ROWS), 1) < 2
    for which, rows in enumerate((key * value, grad * query)):
        turned = jnp.concatenate([rows, below], axis=0).astype(jnp.bfloat16).T
        kept = rough_ref[:, which].reshape(block, ROWS)
        out_ref[:, which] = jnp.where(head, turned, kept).reshape(per, width, ROWS)


def headed(rough, proj, edge, taps, grad_out):
    channels = proj.shape[-1]
    width = rough.shape[2]
    block = min(2048, channels)
    shape = (block // width, 2, width, ROWS)
    return pl.pallas_call(
        head_kernel,
        grid=(channels // block,),
        in_specs=[
            pl.BlockSpec(shape, lambda i: (i, 0, 0, 0)),
            pl.BlockSpec((3, 16, block), lambda i: (0, 0, i)),
            pl.BlockSpec((8, block), lambda i: (0, i)),
            pl.BlockSpec((3, 3, block), lambda i: (0, 0, i)),
            pl.BlockSpec((16, block), lambda i: (0, i)),
        ],
        out_specs=pl.BlockSpec(shape, lambda i: (i, 0, 0, 0)),
        out_shape=pltpu.HBM(rough.shape, jnp.bfloat16),
        compiler_params=params(32),
    )(rough, held(proj), edge, taps, held(grad_out))


def spectrum_kernel(filter_ref, fwd_a_ref, turn_ref, fwd_b_ref, out_ref):
    cos_w, sin_w = turn_ref[0], turn_ref[1]

    def one(ch, carry):
        high, low = split(filter_ref[ch])
        y = dot(fwd_a_ref[...], jnp.concatenate([high, high], axis=0))
        y += dot(fwd_a_ref[...], jnp.concatenate([low, low], axis=0))
        y_re, y_im = y[:ROWS], y[ROWS:]
        turned = jnp.concatenate(
            [y_re * cos_w - y_im * sin_w, y_re * sin_w + y_im * cos_w], axis=1
        )
        high, low = split(turned)
        out_ref[ch] = dot(high, fwd_b_ref[0]) + dot(high, fwd_b_ref[1]) + dot(low, fwd_b_ref[0])
        return carry

    lax.fori_loop(0, filter_ref.shape[0], one, 0, unroll=2)


def whole(shape):
    return pl.BlockSpec(shape, lambda *_: (0,) * len(shape))


def spectrum(filter_sq, tab):
    width = filter_sq.shape[0]
    block = min(8, width)
    return pl.pallas_call(
        spectrum_kernel,
        grid=(width // block,),
        in_specs=[
            pl.BlockSpec((block, ROWS, ROWS), lambda i: (i, 0, 0)),
            whole((2 * ROWS, 2 * ROWS)),
            whole((2, ROWS, ROWS)),
            whole((2, 2 * ROWS, 2 * ROWS)),
        ],
        out_specs=pl.BlockSpec((block, ROWS, 2 * ROWS), lambda i: (i, 0, 0)),
        out_shape=pltpu.HBM((width, ROWS, 2 * ROWS), jnp.float32),
        compiler_params=params(32),
        cost_estimate=pl.CostEstimate(
            flops=width * 5 * 2 * (2 * ROWS) ** 3, bytes_accessed=width * 3 * 4 * ROWS**2,
            transcendentals=0,
        ),
    )(filter_sq, tab["fwd_a"], tab["turn"], tab["fwd_b"])


def apply_right(rows, table_ref):
    total = dot(rows, table_ref[0])
    for term in range(1, table_ref.shape[0]):
        total += dot(rows, table_ref[term])
    return total


def apply_left(table_ref, columns):
    total = dot(table_ref[0], columns)
    for term in range(1, table_ref.shape[0]):
        total += dot(table_ref[term], columns)
    return total


def side(left, right):
    return jnp.concatenate([left.astype(jnp.bfloat16), right.astype(jnp.bfloat16)], axis=1)


def turned_back(spectra, inv_b_ref, inv_a_ref, cos_w, sin_w):
    v = apply_right(spectra, inv_b_ref)
    parts_re, parts_im = [], []
    for at in range(spectra.shape[0] // ROWS):
        v_re, v_im = halves(v[at * ROWS : (at + 1) * ROWS])
        parts_re.append((v_re * cos_w + v_im * sin_w).astype(jnp.bfloat16))
        parts_im.append((v_im * cos_w - v_re * sin_w).astype(jnp.bfloat16))
    parts = [jnp.concatenate(parts_re, axis=1), jnp.concatenate(parts_im, axis=1)]
    return apply_left(inv_a_ref, jnp.concatenate(parts, axis=0))


def conv_kernel(
    in_ref, spec_ref, fwd_a_ref, turn_ref, fwd_b_ref, inv_b_ref, inv_a_ref,
    out_ref, lag_ref, rows_ref, outs_ref, *, group,
):
    block = out_ref.shape[2]
    pitch = rows_ref.shape[1] // ROWS
    part = pl.program_id(1)
    here = pl.ds(pl.multiple_of(pl.program_id(0) * block, block), block)

    @pl.when(part == 0)
    def _():
        for at in range(2):
            rows = in_ref[:, at, here].astype(jnp.float32)
            spare = jnp.zeros((ROWS, pitch - block, ROWS), jnp.float32)
            rows_ref[at] = jnp.concatenate([rows, spare], axis=1).reshape(ROWS * pitch, ROWS)

    cos_w, sin_w = turn_ref[0], turn_ref[1]

    def some():
        chans = [part * group + at for at in range(group)]
        places = [(at, pl.ds(ch, ROWS, stride=pitch)) for ch in chans for at in range(2)]
        rows = [rows_ref[at, strided, :].astype(jnp.bfloat16) for at, strided in places]
        columns = jnp.concatenate(rows, axis=1)
        y = dot(fwd_a_ref[...], jnp.concatenate([columns, columns], axis=0))
        turned = []
        for at in range(2 * group):
            y_re = y[:ROWS, at * ROWS : (at + 1) * ROWS]
            y_im = y[ROWS:, at * ROWS : (at + 1) * ROWS]
            turned.append(side(y_re * cos_w - y_im * sin_w, y_re * sin_w + y_im * cos_w))
        z = apply_right(jnp.concatenate(turned, axis=0), fwd_b_ref)
        products = []
        for at in range(group):
            x_re, x_im = halves(z[2 * at * ROWS : (2 * at + 1) * ROWS])
            g_re, g_im = halves(z[(2 * at + 1) * ROWS : (2 * at + 2) * ROWS])
            h_re, h_im = halves(spec_ref[at])
            lag_ref[at] = side(g_re * x_re + g_im * x_im, g_im * x_re - g_re * x_im)
            products.append(side(x_re * h_re - x_im * h_im, x_re * h_im + x_im * h_re))
            products.append(side(h_re * g_re + h_im * g_im, h_re * g_im - h_im * g_re))
        res = turned_back(jnp.concatenate(products, axis=0), inv_b_ref, inv_a_ref, cos_w, sin_w)
        for column, (at, strided) in enumerate(places):
            outs_ref[at, strided, :] = res[:, column * ROWS : (column + 1) * ROWS]

    some()

    @pl.when(part == pl.num_programs(1) - 1)
    def _():
        for at in range(2):
            rows = outs_ref[at].reshape(ROWS, pitch, ROWS)[:, :block]
            out_ref[:, at] = rows.astype(jnp.bfloat16)


def convolve(received, spec, tab, group=8, block=16):
    width = received.shape[2]
    names = ("fwd_a", "turn", "fwd_b_high", "inv_b_high", "inv_a_high")
    return pl.pallas_call(
        functools.partial(conv_kernel, group=group),
        grid=(width // block, block // group),
        in_specs=[
            pl.BlockSpec(memory_space=pltpu.VMEM),
            pl.BlockSpec((group, ROWS, 2 * ROWS), lambda i, j: (i * (block // group) + j, 0, 0)),
        ]
        + [whole(tab[name].shape) for name in names],
        out_specs=[
            pl.BlockSpec((ROWS, 2, block, ROWS), lambda i, j: (0, 0, i, 0)),
            pl.BlockSpec((group, ROWS, 2 * ROWS), lambda i, j: (i * (block // group) + j, 0, 0)),
        ],
        out_shape=[
            pltpu.HBM((ROWS, 2, width, ROWS), jnp.bfloat16),
            pltpu.HBM((width, ROWS, 2 * ROWS), jnp.bfloat16),
        ],
        scratch_shapes=[pltpu.VMEM((2, ROWS * (block + 8), ROWS), jnp.float32)] * 2,
        compiler_params=params(40),
    )(received, held(spec), *(tab[name] for name in names))


def lag_kernel(products_ref, turn_ref, inv_b_ref, inv_a_ref, out_ref):
    count = products_ref.shape[0]
    products = products_ref[...].reshape(count * ROWS, 2 * ROWS)
    res = turned_back(products, inv_b_ref, inv_a_ref, turn_ref[0], turn_ref[1])
    for ch in range(count):
        out_ref[ch] = res[:, ch * ROWS : (ch + 1) * ROWS]


def lags(products, tab):
    width = products.shape[0]
    block = min(8, width)
    names = ("turn", "inv_b", "inv_a")
    return pl.pallas_call(
        lag_kernel,
        grid=(width // block,),
        in_specs=[pl.BlockSpec((block, ROWS, 2 * ROWS), lambda i: (i, 0, 0))]
        + [whole(tab[name].shape) for name in names],
        out_specs=pl.BlockSpec((block, ROWS, ROWS), lambda i: (i, 0, 0)),
        out_shape=jax.ShapeDtypeStruct((width, ROWS, ROWS), jnp.float32),
        compiler_params=params(32),
        cost_estimate=pl.CostEstimate(
            flops=width * 4 * 2 * (2 * ROWS) ** 3, bytes_accessed=width * 8 * ROWS**2,
            transcendentals=0,
        ),
    )(products, *(tab[name] for name in names))


def fill_turned(turned_ref, ret_ref):
    block = turned_ref.shape[2]
    for at in range(2):
        turned_ref[at] = ret_ref[:, at].reshape(block, ROWS).T.astype(jnp.float32)


def grads_at(turned_ref, taps_ref, grad_ref, row, lanes, keys, values):
    rows = pl.ds(row, STEP)
    conv, corr = turned_ref[0, rows, lanes], turned_ref[1, rows, lanes]
    key = filtered(taps_ref, 1, lanes, keys)
    value = filtered(taps_ref, 2, lanes, values)
    return (grad_ref[rows, lanes].astype(jnp.float32) * conv, corr * value, corr * key)


def sums_kernel(
    ret_ref, proj_ref, edge_ref, taps_ref, grad_ref, sums_ref, first_ref, ext_ref, turned_ref
):
    block = grad_ref.shape[1]
    channels = pl.ds(pl.multiple_of(pl.program_id(0) * block, block), block)
    fill_ext(ext_ref, proj_ref.at[:, :, channels], edge_ref)
    per = ROWS // ret_ref.shape[2]
    first_ref[...] = jnp.zeros_like(first_ref)
    sums_ref[...] = jnp.zeros_like(sums_ref)
    for at, lanes in enumerate(lanes_of(grad_ref.shape[1])):
        sums = [jnp.zeros((8, ROWS), jnp.float32)] * 9
        for which in range(2):
            turned = ret_ref[pl.ds(at * per, per), which].reshape(ROWS, ROWS).T
            turned_ref[which, :, lanes] = turned.astype(jnp.float32)
        for row in range(0, ROWS, STEP):
            shifted = [inputs_at(ext_ref, stream, row, lanes) for stream in range(3)]
            grads = grads_at(turned_ref, taps_ref, grad_ref, row, lanes, shifted[1], shifted[2])
            for stream in range(3):
                for tap in range(3):
                    terms = (grads[stream] * shifted[stream][tap]).reshape(STEP // 8, 8, ROWS)
                    sums[3 * stream + tap] = sums[3 * stream + tap] + jnp.sum(terms, axis=0)
                if row == 0:
                    first_ref[pl.ds(2 * stream, 2), lanes] = grads[stream][:2]
        for which in range(9):
            sums_ref[which, pl.ds(at, 1)] = jnp.sum(sums[which], axis=0, keepdims=True)


def local_specs(block, width):
    return [
        pl.BlockSpec((block // width, 2, width, ROWS), lambda i: (i, 0, 0, 0)),
        pl.BlockSpec((3, ROWS, block), lambda i: (0, 0, i)),
        pl.BlockSpec((8, block), lambda i: (0, i)),
        pl.BlockSpec((3, 3, block), lambda i: (0, 0, i)),
        pl.BlockSpec((ROWS, block), lambda i: (0, i)),
    ]


def tap_sums(returned, proj, edge, taps, grad_out):
    channels = proj.shape[-1]
    block = min(1024, channels)
    specs = local_specs(block, returned.shape[2])
    specs[1] = pl.BlockSpec(memory_space=pltpu.VMEM)
    return pl.pallas_call(
        sums_kernel,
        grid=(channels // block,),
        in_specs=specs,
        out_specs=[
            pl.BlockSpec((16, block // ROWS, ROWS), lambda i: (0, i, 0)),
            pl.BlockSpec((8, block), lambda i: (0, i)),
        ],
        out_shape=[
            pltpu.HBM((16, channels // ROWS, ROWS), jnp.float32),
            pltpu.HBM((8, channels), jnp.float32),
        ],
        scratch_shapes=[
            pltpu.VMEM((3, ROWS + 8, block), jnp.float32),
            pltpu.VMEM((2, ROWS, block), jnp.float32),
        ],
        compiler_params=params(40),
    )(returned, proj, edge, taps, held(grad_out))


def grads_kernel(
    ret_ref, proj_ref, edge_ref, taps_ref, grad_ref, later_ref,
    out_ref, ext_ref, turned_ref, grads_ref,
):
    fill_ext(ext_ref, proj_ref, edge_ref)
    fill_turned(turned_ref, ret_ref)
    for stream in range(3):
        grads_ref[stream, pl.ds(ROWS, 2), :] = later_ref[pl.ds(2 * stream, 2), :]
    for lanes in lanes_of(grad_ref.shape[1]):
        for row in range(0, ROWS, STEP):
            shifted = [inputs_at(ext_ref, stream, row, lanes) for stream in (1, 2)]
            grads = grads_at(turned_ref, taps_ref, grad_ref, row, lanes, *shifted)
            for stream in range(3):
                grads_ref[stream, pl.ds(row, STEP), lanes] = grads[stream]
        for stream in range(3):
            for row in range(0, ROWS, STEP):
                ahead = [grads_ref[stream, pl.ds(row + tap, STEP), lanes] for tap in range(3)]
                total = filtered(taps_ref, stream, lanes, ahead)
                out_ref[stream, pl.ds(row, STEP), lanes] = total.astype(jnp.bfloat16)


def stream_grads(returned, proj, edge, taps, grad_out, later):
    channels = proj.shape[-1]
    block = min(1024, channels)
    return pl.pallas_call(
        grads_kernel,
        grid=(channels // block,),
        in_specs=local_specs(block, returned.shape[2])
        + [pl.BlockSpec((8, block), lambda i: (0, i))],
        out_specs=pl.BlockSpec((3, ROWS, block), lambda i: (0, 0, i)),
        out_shape=jax.ShapeDtypeStruct((3, ROWS, channels), jnp.bfloat16),
        scratch_shapes=[
            pltpu.VMEM((3, ROWS + 8, block), jnp.float32),
            pltpu.VMEM((2, ROWS, block), jnp.float32),
            pltpu.VMEM((3, ROWS + 8, block), jnp.float32),
        ],
        compiler_params=params(40),
        cost_estimate=pl.CostEstimate(
            flops=60 * ROWS * channels, bytes_accessed=18 * ROWS * channels, transcendentals=0
        ),
    )(returned, held(proj), edge, taps, held(grad_out), later)


def passed_along(value, steps):
    count = lax.axis_size("ctx")
    initial, last = (max(0, -steps), min(count, count - steps))
    return lax.ppermute(value, "ctx", [(source, source + steps) for source in range(initial, last)])


def exchanged(value, axes):
    return lax.all_to_all(value, axes, split_axis=0, concat_axis=0, tiled=True)


def sum_everywhere(sums, beside):
    channels = sums.shape[1] * ROWS
    devices = lax.axis_size("dp") * lax.axis_size("ctx")
    pieces = sums.reshape(devices, 2, ROWS)
    own = jnp.sum(exchanged(pieces, ("dp", "ctx")), axis=0)
    own, beside = lax.optimization_barrier((own.astype(jnp.bfloat16), beside))
    spread = exchanged(jnp.broadcast_to(own[None], pieces.shape), ("dp", "ctx"))
    return spread.reshape(16, channels)[:9].reshape(3, 3, channels).astype(jnp.float32), beside


def local(projected, short_taps, long_filter, grad_out):
    tab = tables()
    proj = projected[:, 0]
    grad_rows = grad_out[0]
    width = long_filter.shape[0]
    edge = passed_along(edges(proj), 1)
    rough = gates(proj, short_taps, grad_rows, width)
    sent = headed(rough, proj, edge, short_taps, grad_rows)
    received = exchanged(sent, "ctx")
    spec = spectrum(long_filter.reshape(width, ROWS, ROWS), tab)
    results, products = convolve(received, spec, tab)
    returned = exchanged(results, "ctx")
    lag = lags(products, tab)
    second = lax.axis_index("dp") == 1
    lower, upper = lag[:, : ROWS // 2], lag[:, ROWS // 2 :]
    other = lax.ppermute(
        jnp.where(second, lower, upper).astype(jnp.bfloat16), "dp", [(0, 1), (1, 0)]
    )
    lag_sum = jnp.where(second, upper, lower) + other.astype(jnp.float32)
    grad_filter = lag_sum.reshape(width, ROWS // 2 * ROWS)
    late_edge, grad_filter = lax.optimization_barrier((edge, grad_filter))
    sums, first = tap_sums(returned, proj, late_edge, short_taps, grad_rows)
    grad_taps, later = sum_everywhere(sums, passed_along(first, -1))
    grad_in = stream_grads(returned, proj, edge, short_taps, grad_rows, later)
    return (grad_in[:, None], grad_taps, grad_filter)


def solution(mesh):
    return jax.shard_map(
        local,
        mesh=mesh,
        in_specs=(P(None, "dp", "ctx", None), P(), P("ctx", None), P("dp", "ctx", None)),
        out_specs=(P(None, "dp", "ctx", None), P(), P("ctx", "dp")),
        check_vma=False,
    )
```
